1024 devices in a mesh: gx: 16 (over x, z_lo), gy: 4 (over z_hi), gz: 16 (over y, core).
Axes of the slice: x: 4, y: 8, z: 16 (z_hi: 4, z_lo: 4; z = z_hi * 4 + z_lo), core: 2. Of those that a mesh axis runs over, the one named last changes fastest.
Arguments:
- vel_x: float32 [256, 128, 512], P('gx', 'gz', 'gy'), may hold values from -6 to 6
- vel_y: float32 [256, 128, 512], P('gx', 'gz', 'gy'), may hold values from -6 to 6
- vel_z: float32 [256, 128, 512], P('gx', 'gz', 'gy'), may hold values from -6 to 6
- pressure: float32 [256, 128, 512], P('gx', 'gz', 'gy'), may hold values from -6 to 6
- phase: int32 [256, 128, 512], P('gx', 'gz', 'gy'), may hold values from 0 to 3
- visc_scale: float32 [4], replicated, may hold values from 0.5 to 2
- power_n: float32 [4], replicated, may hold values from 1 to 4
- density: float32 [4], replicated, may hold values from 0.5 to 1.5
Outputs:
- out_vx: float32 [256, 128, 512], P('gx', 'gz', 'gy')
- out_vy: float32 [256, 128, 512], P('gx', 'gz', 'gy')
- out_vz: float32 [256, 128, 512], P('gx', 'gz', 'gy')
- out_p: float32 [256, 128, 512], P('gx', 'gz', 'gy')
- out_eta: float32 [256, 128, 512], P('gx', 'gz', 'gy')
The draws below stay inside these ranges and needn't reach their ends.
All inputs are finite; a program needn't handle non-finite values.
Results may differ from the reference program's by a relative error of at most 0.00013.
Values sent between devices are 32-bit elements; how exact they have to be, the bound alone decides.
A program may use at most 32 MiB of HBM per device.

```python
import math
import jax
import jax.numpy as jnp
from jax import lax

ITERS = 4
PHASES = 4
NX = 256
NZ = 128
NY = 512


def plant(drawn, key, smallest, largest):
    longest = drawn.shape.index(max(drawn.shape))
    spots = []
    for shift in (0, 1):
        where = [jax.random.randint(jax.random.fold_in(key, axis), (), 0, length) for axis, length in enumerate(drawn.shape)]
        where[longest] = (where[longest] + shift) % drawn.shape[longest]
        spots.append(tuple(where))
    return drawn.at[spots[0]].set(smallest).at[spots[1]].set(largest)


def block_levels(stream_key, shape, cuts, low, high):
    loudness, own = 1.0, jax.random.fold_in(stream_key, 6)
    for position, blocks in cuts:
        steps = jnp.exp(jax.random.uniform(jax.random.fold_in(own, position), (blocks,), jnp.float32, low / len(cuts), high / len(cuts)))
        loudness = loudness * jnp.repeat(steps, shape[position] // blocks).reshape([-1 if axis == position else 1 for axis in range(len(shape))])
    return loudness


def normal_values(rng, dims, width, reach, split=(), dtype=jnp.bfloat16):
    drawn = jax.random.normal(rng, dims, jnp.float32) * width
    if len(split) > 0:
        drawn = block_levels(rng, dims, split, -0.22, 0.18) * drawn
    return jnp.clip(drawn, min=-reach, max=reach).astype(dtype)


def setup_inputs(seed: int = 0) -> dict:
    key_of = jax.random.split(jax.random.key(seed), 9)
    vel_x = normal_values(key_of[0], (NX, NZ, NY), 1.0, 6.0, ((0, 16), (1, 16), (2, 4)), jnp.float32)
    vel_y = normal_values(key_of[1], (NX, NZ, NY), 1.0, 6.0, ((0, 16), (1, 16), (2, 4)), jnp.float32)
    vel_z = normal_values(key_of[2], (NX, NZ, NY), 1.0, 6.0, ((0, 16), (1, 16), (2, 4)), jnp.float32)
    pressure = normal_values(key_of[3], (NX, NZ, NY), 1.0, 6.0, ((0, 16), (1, 16), (2, 4)), jnp.float32)
    phase = plant(jax.random.randint(key_of[4], (NX, NZ, NY), 0, PHASES), jax.random.fold_in(key_of[4], 1), 0, PHASES - 1).astype(jnp.int32)
    visc_scale = jnp.clip(jnp.exp(jax.random.uniform(key_of[5], (PHASES,), jnp.float32, math.log(0.5), math.log(2.0))), 0.5, 2.0)
    power_n = jnp.clip(jax.random.uniform(key_of[6], (PHASES,), jnp.float32, 1.0, 4.0), 1.0, 4.0)
    density = jnp.clip(jax.random.uniform(key_of[7], (PHASES,), jnp.float32, 0.5, 1.5), 0.5, 1.5)
    return {"vel_x": vel_x, "vel_y": vel_y, "vel_z": vel_z, "pressure": pressure, "phase": phase, "visc_scale": visc_scale, "power_n": power_n, "density": density}


strain_floor = 1.0
pressure_step = 0.5
velocity_step = 0.1


def lookup(phase, table):
    out = jnp.zeros(phase.shape, jnp.float32)
    for index in range(PHASES):
        out = out + jnp.where(phase == index, table[index], jnp.float32(0.0))
    return out


def strain_rate_list(padded):
    strain_rate_first = padded[0, 2:, 1:-1, 1:-1] - padded[0, 1:-1, 1:-1, 1:-1]
    strain_rate_second = padded[1, 1:-1, 2:, 1:-1] - padded[1, 1:-1, 1:-1, 1:-1]
    strain_rate_third = padded[2, 1:-1, 1:-1, 2:] - padded[2, 1:-1, 1:-1, 1:-1]
    return strain_rate_first, strain_rate_second, strain_rate_third


def viscosity(strain_rate_first, strain_rate_second, strain_rate_third, prefactor, exponent):
    div = strain_rate_first + strain_rate_second + strain_rate_third
    third = div / 3.0
    inv = 0.5 * ((strain_rate_first - third) ** 2 + (strain_rate_second - third) ** 2 + (strain_rate_third - third) ** 2) + strain_floor
    eta = prefactor * jnp.exp(0.5 * (1.0 / exponent - 1.0) * jnp.log(inv))
    return eta, div


def slice_along(field, offset, grid_extent):
    return field[1 + offset[0]:1 + offset[0] + grid_extent[0], 1 + offset[1]:1 + offset[1] + grid_extent[1], 1 + offset[2]:1 + offset[2] + grid_extent[2]]


def unit(sweep_heading, sign):
    offset = [0, 0, 0]
    offset[sweep_heading] = sign
    return tuple(offset)


def joined(first, second):
    return tuple(first[n] + second[n] for n in range(3))


def residual_field(sweep_heading, padded_velocity, padded_pressure, padded_viscosity, grid_extent):
    zero_scalar = (0, 0, 0)
    backward_neighbor = unit(sweep_heading, -1)
    middle_slice = slice_along(padded_velocity, zero_scalar, grid_extent)
    viscosity_current = slice_along(padded_viscosity, zero_scalar, grid_extent)
    viscosity_backward = slice_along(padded_viscosity, backward_neighbor, grid_extent)
    momentum_residual = -(slice_along(padded_pressure, zero_scalar, grid_extent) - slice_along(padded_pressure, backward_neighbor, grid_extent))
    for other in range(3):
        upper_neighbor = unit(other, 1)
        lower_neighbor = unit(other, -1)
        if other == sweep_heading:
            momentum_residual = momentum_residual + viscosity_current * (slice_along(padded_velocity, upper_neighbor, grid_extent) - middle_slice) - viscosity_backward * (middle_slice - slice_along(padded_velocity, backward_neighbor, grid_extent))
        else:
            viscosity_above = 0.25 * (viscosity_current + viscosity_backward + slice_along(padded_viscosity, upper_neighbor, grid_extent) + slice_along(padded_viscosity, joined(backward_neighbor, upper_neighbor), grid_extent))
            viscosity_below = 0.25 * (viscosity_current + viscosity_backward + slice_along(padded_viscosity, lower_neighbor, grid_extent) + slice_along(padded_viscosity, joined(backward_neighbor, lower_neighbor), grid_extent))
            momentum_residual = momentum_residual + viscosity_above * (slice_along(padded_velocity, upper_neighbor, grid_extent) - middle_slice) - viscosity_below * (middle_slice - slice_along(padded_velocity, lower_neighbor, grid_extent))
    return momentum_residual, 0.5 * (viscosity_current + viscosity_backward)


def reference(vel_x, vel_y, vel_z, pressure, phase, visc_scale, power_n, density):
    grid_extent = pressure.shape
    coords = [lax.broadcasted_iota(jnp.int32, grid_extent, axis_number) for axis_number in range(3)]
    velocity = [jnp.where(coords[axis_number] == 0, jnp.float32(0.0), v) for axis_number, v in enumerate((vel_x, vel_z, vel_y))]
    prefactor = lookup(phase, visc_scale)
    exponent = lookup(phase, power_n)
    rho = lookup(phase, density)
    total_cells = float(grid_extent[0] * grid_extent[1] * grid_extent[2])
    eta = prefactor
    for step in range(ITERS):
        stacked_rates = jnp.pad(jnp.stack(velocity), ((0, 0), (1, 1), (1, 1), (1, 1)))
        strain_rate_first, strain_rate_second, strain_rate_third = strain_rate_list(stacked_rates)
        eta, div = viscosity(strain_rate_first, strain_rate_second, strain_rate_third, prefactor, exponent)
        pressure = pressure - pressure_step * eta * div
        pressure = pressure - jnp.sum(pressure) / total_cells
        padded_pressure = jnp.pad(pressure, 1)
        padded_viscosity = jnp.pad(eta, 1)
        updated = []
        for axis_number in range(3):
            momentum_residual, face_slice = residual_field(axis_number, stacked_rates[axis_number], padded_pressure, padded_viscosity, grid_extent)
            if axis_number == 1:
                momentum_residual = momentum_residual - rho
            fresh = velocity[axis_number] + velocity_step * momentum_residual / face_slice
            updated.append(jnp.where(coords[axis_number] == 0, jnp.float32(0.0), fresh))
        velocity = updated
    return velocity[0], velocity[2], velocity[1], pressure, eta
```

```python
import functools

import jax
import jax.numpy as jnp
from jax import lax
from jax.experimental import pallas as pl
from jax.experimental.pallas import tpu as pltpu
from jax.sharding import PartitionSpec as P

ITERS = 4
PHASES = 4
STRAIN_FLOOR = 1.0
PRESSURE_STEP = 0.5
VELOCITY_STEP = 0.1

BX, BZ, BY = 16, 8, 128
LOW, HIGH = 2, 4
YLOW, YHIGH = 4, 8
PLANES = BX + LOW + HIGH
ROWS = 2 * BZ
GROUP = YLOW + YHIGH
Z_LO = 4
MESH = pl.DeviceIdType.MESH

SIDES = tuple((a, b) for a in (-1, 0, 1) for b in (-1, 0, 1) if (a, b) != (0, 0))


def send_planes(a):
    return {0: (LOW, BX), 1: (LOW + BX - LOW, LOW), -1: (LOW, HIGH)}[a]


def land_planes(a):
    return {0: LOW, 1: 0, -1: LOW + BX}[a]


def send_rows(b):
    return {0: (0, BZ), 1: (BZ - LOW, LOW), -1: (0, HIGH)}[b]


def land_rows(b):
    return {0: 0, 1: ROWS - LOW, -1: BZ}[b]


def y_roll(x, s):
    r = pltpu.roll(x, s % BY, 1)
    swapped = jnp.concatenate([r[ROWS:], r[:ROWS]], axis=0)
    lane = lax.broadcasted_iota(jnp.int32, x.shape, 1)
    return jnp.where(lane == (0 if s == 1 else BY - 1), swapped, r)


def z_roll(x, s):
    return jnp.concatenate(
        [pltpu.roll(x[:ROWS], s % ROWS, 0), pltpu.roll(x[ROWS:], s % ROWS, 0)], axis=0
    )


def kernel(sizes, vx_ref, vy_ref, vz_ref, p_ref, ph_ref, vs_ref, pn_ref, dn_ref, out_ref,
           ph_in, first, second, s_pack, r_pack, vel, pres, pref, expo, rho, eta_out, ar_src, ar_buf,
           in_sem, ysend, yrecv, send_a, recv_a, send_b, recv_b, send_c, recv_c, ar_send, ar_recv):
    ngx, ngy, ngz, z_lo = sizes
    gx, gy, gz = lax.axis_index("gx"), lax.axis_index("gy"), lax.axis_index("gz")
    n_x, n_z = ngx // z_lo, z_lo * ngy

    in_copies = []
    for n, (src, dst) in enumerate(
        ((vx_ref, first.at[0, pl.ds(LOW, BX), pl.ds(0, BZ)]),
         (vz_ref, first.at[1, pl.ds(LOW, BX), pl.ds(0, BZ)]),
         (vy_ref, first.at[2, pl.ds(LOW, BX), pl.ds(0, BZ)]),
         (p_ref, first.at[3, pl.ds(LOW, BX), pl.ds(0, BZ)]),
         (ph_ref, ph_in))):
        cp = pltpu.make_async_copy(src, dst, in_sem.at[n])
        cp.start()
        in_copies.append(cp)

    def neighbour(a, b, c):
        return (lax.rem(gx + (a + ngx), ngx), lax.rem(gy + (c + ngy), ngy), lax.rem(gz + (b + ngz), ngz))

    def along_gz(o):
        return (gx, gy, lax.rem(gz + o, ngz))

    def along_x(o):
        return (lax.rem(gx + o * z_lo, ngx), gy, gz)

    z_here = gy * z_lo + lax.rem(gx, z_lo)

    def along_z(o):
        z = lax.rem(z_here + o, n_z)
        return (gx - lax.rem(gx, z_lo) + lax.rem(z, z_lo), z // z_lo, gz)

    sum_phases = (
        [along_gz(o) for o in range(1, ngz)],
        [along_x(o) for o in range(1, n_x)],
        [along_z(o) for o in range(1, n_z)],
    )

    barrier = pltpu.get_barrier_semaphore()
    greeted = [neighbour(a, b, 0) for a, b in SIDES] + [neighbour(0, 0, -1), neighbour(0, 0, 1)]
    greeted += [d for group in sum_phases for d in group]
    for d in greeted:
        pl.semaphore_signal(barrier, inc=1, device_id=d, device_id_type=MESH)

    lane_v = lax.broadcasted_iota(jnp.int32, (BZ, BY), 1)
    for cp in in_copies:
        cp.wait()
    first[4, LOW:LOW + BX, 0:BZ] = ph_in[...].astype(jnp.float32)

    def pack(k, carry):
        lo = jnp.zeros((BZ, BY), jnp.float32)
        hi = jnp.zeros((BZ, BY), jnp.float32)
        for q in range(2):
            for a in range(5):
                base = GROUP * a + 64 * q
                rolled = first[a, LOW + 2 * k + q, 0:BZ]
                if base:
                    rolled = pltpu.roll(rolled, base, 1)
                lo = jnp.where((lane_v >= base) & (lane_v < base + YHIGH), rolled, lo)
                if base:
                    hi = jnp.where((lane_v >= base - YLOW) & (lane_v < base), rolled, hi)
                else:
                    hi = jnp.where(lane_v >= BY - YLOW, rolled, hi)
        s_pack[0, k] = lo
        s_pack[1, k] = hi
        return carry

    lax.fori_loop(0, BX // 2, pack, 0)
    pl.semaphore_wait(barrier, len(greeted))

    y_copies = []
    for n, c in enumerate((-1, 1)):
        cp = pltpu.make_async_remote_copy(
            src_ref=s_pack.at[n], dst_ref=r_pack.at[n], send_sem=ysend.at[n], recv_sem=yrecv.at[n],
            device_id=neighbour(0, 0, c), device_id_type=MESH)
        cp.start()
        y_copies.append(cp)

    def exchange(buf, lo, count, send, recv):
        copies = []
        for n, (a, b) in enumerate(SIDES):
            (p0, pn), (r0, rn) = send_planes(a), send_rows(b)
            cp = pltpu.make_async_remote_copy(
                src_ref=buf.at[pl.ds(lo, count), pl.ds(p0, pn), pl.ds(r0, rn)],
                dst_ref=buf.at[pl.ds(lo, count), pl.ds(land_planes(a), pn), pl.ds(land_rows(b), rn)],
                send_sem=send.at[n], recv_sem=recv.at[n],
                device_id=neighbour(a, b, 0), device_id_type=MESH)
            cp.start()
            copies.append(cp)
        return copies

    main_copies = exchange(first, 0, 5, send_a, recv_a)
    for cp in y_copies:
        cp.wait_recv()

    def unpack_y(k, carry):
        low_lane = lax.rem(lane_v + YLOW, 64)
        from_low = lax.rem(low_lane, GROUP) < YLOW
        both = jnp.where(from_low, r_pack[1, k], r_pack[0, k])
        first[5, LOW + 2 * k, 0:BZ] = both
        first[5, LOW + 2 * k + 1, 0:BZ] = pltpu.roll(both, 64, 1)
        return carry

    lax.fori_loop(0, BX // 2, unpack_y, 0)
    halo_copies = exchange(first, 5, 1, send_b, recv_b)
    for cp in main_copies + halo_copies:
        cp.wait_recv()

    full = (2 * ROWS, BY)
    row = lax.broadcasted_iota(jnp.int32, full, 0)
    lane = lax.broadcasted_iota(jnp.int32, full, 1)
    half = row // ROWS
    zr = row - half * ROWS
    zi = gz * BZ + jnp.where(zr >= ROWS - LOW, zr - ROWS, zr)
    yi = gy * BY + jnp.where(half == 0, lane, jnp.where(lane >= BY // 2, lane - BY, lane + BY))
    in_zy = (zi >= 0) & (zi < ngz * BZ) & (yi >= 0) & (yi < ngy * BY)
    in_z1 = in_zy & (zi >= 1)
    in_y1 = in_zy & (yi >= 1)

    def x_of(j):
        return gx * BX - LOW + j

    def inside(j, comp):
        xi = x_of(j)
        high = xi < ngx * BX
        if comp == 0:
            return in_zy & ((xi >= 1) & high)
        return {1: in_z1, 2: in_y1, None: in_zy}[comp] & ((xi >= 0) & high)

    def whole(buf, count, a, j):
        packed = buf[count, j]
        halo = pltpu.roll(packed, BY - GROUP * a, 1) if a else packed
        return jnp.concatenate([buf[a, j], halo], axis=0)

    def lookup_rows(ref):
        return [jnp.full(full, ref[k], jnp.float32) for k in range(PHASES)]

    scales, powers, densities = lookup_rows(vs_ref), lookup_rows(pn_ref), lookup_rows(dn_ref)
    powers = [0.5 * (1.0 / n - 1.0) for n in powers]

    def select(phase, table):
        out = table[PHASES - 1]
        for k in range(PHASES - 2, -1, -1):
            out = jnp.where(phase == float(k), table[k], out)
        return out

    def unpack_first(j, carry):
        for a in range(3):
            vel[a, j + 1] = jnp.where(inside(j, a), whole(first, 5, a, j), 0.0)
        pres[j] = whole(first, 5, 3, j)
        phase = whole(first, 5, 4, j)
        pref[j] = jnp.where(inside(j, None), select(phase, scales), 0.0)
        expo[j] = select(phase, powers)
        rho[j] = select(phase, densities)
        return carry

    lax.fori_loop(0, PLANES, unpack_first, 0)

    def iteration(first_plane, last_plane, keep_eta):
        zero = jnp.zeros(full, jnp.float32)

        def stage(j, carry):
            eta_m, tx_m, vz_m, vy_m, fzx_m, fyx_m, pz_m, py_m, az_m, ay_m, rho_m = carry
            vx, vz, vy = vel[0, j + 1], vel[1, j + 1], vel[2, j + 1]
            rx = vel[0, j + 2] - vx
            rz = z_roll(vz, -1) - vz
            ry = y_roll(vy, -1) - vy
            div = rx + ry + rz
            third = div * (1.0 / 3.0)
            dx, dy, dz = rx - third, ry - third, rz - third
            inv = 0.5 * (dx * dx + dy * dy + dz * dz) + STRAIN_FLOOR
            eta = pref[j] * jnp.exp(expo[j] * jnp.log(inv))
            p = pres[j] - PRESSURE_STEP * eta * div
            pres[j] = p
            if keep_eta:
                eta_out[j] = eta[0:BZ]
            tx, tz, ty = eta * rx - p, eta * rz - p, eta * ry - p
            ax = eta + eta_m
            az = eta + z_roll(eta, 1)
            ay = eta + y_roll(eta, 1)
            exz = ax + z_roll(ax, 1)
            exy = ax + y_roll(ax, 1)
            eyz = ay + z_roll(ay, 1)
            fzx = exz * (vz - vz_m)
            fyx = exy * (vy - vy_m)
            fxz = exz * (vx - z_roll(vx, 1))
            fxy = exy * (vx - y_roll(vx, 1))
            fyz = eyz * (vy - z_roll(vy, 1))
            fzy = eyz * (vz - y_roll(vz, 1))
            res = tx - tx_m + 0.25 * ((z_roll(fxz, -1) - fxz) + (y_roll(fxy, -1) - fxy))
            vel[0, j + 1] = jnp.where(inside(j, 0), vx + (2.0 * VELOCITY_STEP) * res / ax, 0.0)
            res = pz_m + 0.25 * (fzx - fzx_m) - rho_m
            vel[1, j] = jnp.where(inside(j - 1, 1), vz_m + (2.0 * VELOCITY_STEP) * res / az_m, 0.0)
            res = py_m + 0.25 * (fyx - fyx_m)
            vel[2, j] = jnp.where(inside(j - 1, 2), vy_m + (2.0 * VELOCITY_STEP) * res / ay_m, 0.0)
            pz = tz - z_roll(tz, 1) + 0.25 * (y_roll(fzy, -1) - fzy)
            py = ty - y_roll(ty, 1) + 0.25 * (z_roll(fyz, -1) - fyz)
            return eta, tx, vz, vy, fzx, fyx, pz, py, az, ay, rho[j]

        lax.fori_loop(first_plane, last_plane + 1, stage, (zero,) * 11)

    iteration(0, PLANES - 2, False)
    iteration(1, PLANES - HIGH, False)

    own = lax.broadcasted_iota(jnp.int32, (BZ, BY), 1)

    def repack(i, carry):
        packed = jnp.zeros((BZ, BY), jnp.float32)
        for a in range(4):
            block = vel[a, i + LOW + 1] if a < 3 else pres[i + LOW]
            second[a, i + LOW, 0:BZ] = block[0:BZ]
            halo = block[ROWS:ROWS + BZ]
            base = GROUP * a
            if base:
                halo = pltpu.roll(halo, base, 1)
                packed = jnp.where((own >= base - YLOW) & (own < base + YHIGH), halo, packed)
            else:
                packed = halo
        second[4, i + LOW, 0:BZ] = packed
        return carry

    lax.fori_loop(0, BX, repack, 0)
    second_copies = exchange(second, 0, 5, send_c, recv_c)
    for cp in second_copies:
        cp.wait_recv()

    def unpack_second(j, carry):
        for a in range(3):
            vel[a, j + 1] = jnp.where(inside(j, a), whole(second, 4, a, j), 0.0)
        pres[j] = whole(second, 4, 3, j)
        return carry

    lax.fori_loop(0, PLANES, unpack_second, 0)
    iteration(0, PLANES - 2, False)
    iteration(1, PLANES - HIGH, True)

    total = pres[LOW, 0:BZ]
    for i in range(1, BX):
        total = total + pres[LOW + i, 0:BZ]
    base = 0
    sum_sends = []
    for n, group in enumerate(sum_phases):
        count = len(group)
        ar_src[n] = total
        for o, d in enumerate(group):
            pltpu.make_async_remote_copy(
                src_ref=ar_src.at[n], dst_ref=ar_buf.at[base + o], send_sem=ar_send.at[n], recv_sem=ar_recv.at[n],
                device_id=d, device_id_type=MESH).start()
        part = ar_buf.at[pl.ds(base, count)]
        sum_sends.append(pltpu.make_async_copy(part, part, ar_send.at[n]))
        if n == 0:
            out_ref[0] = vel[0, LOW + 1:LOW + 1 + BX, 0:BZ]
            out_ref[1] = vel[2, LOW + 1:LOW + 1 + BX, 0:BZ]
            out_ref[2] = vel[1, LOW + 1:LOW + 1 + BX, 0:BZ]
            out_ref[4] = eta_out[LOW:LOW + BX]
        pltpu.make_async_copy(part, part, ar_recv.at[n]).wait()
        for o in range(count):
            total = total + ar_buf[base + o]
        base += count
    cells = float(ngx * ngy * ngz * BX * BZ * BY)
    mean = jnp.sum(total) / cells
    out_ref[3] = pres[LOW:LOW + BX, 0:BZ] - mean

    for cp in y_copies + main_copies + halo_copies + second_copies:
        cp.wait_send()
    for cp in sum_sends:
        cp.wait()


def split_kernel(in_ref, *outs):
    for n, out in enumerate(outs):
        out[...] = in_ref[n]


def local(sizes, vel_x, vel_y, vel_z, pressure, phase, visc_scale, power_n, density):
    ngx, ngy, ngz, z_lo = sizes
    partners = (ngz - 1) + (ngx // z_lo - 1) + (z_lo * ngy - 1)
    f32 = jnp.float32
    any_spec = pl.BlockSpec(memory_space=pl.ANY)
    smem = pl.BlockSpec(memory_space=pltpu.SMEM)
    vmem = pl.BlockSpec(memory_space=pltpu.VMEM)
    dma = pltpu.SemaphoreType.DMA
    plane = (2 * ROWS, BY)
    stacked = pl.pallas_call(
        functools.partial(kernel, sizes),
        out_shape=jax.ShapeDtypeStruct((5, BX, BZ, BY), f32),
        in_specs=[any_spec] * 5 + [smem] * 3,
        out_specs=vmem,
        scratch_shapes=[
            pltpu.VMEM((BX, BZ, BY), jnp.int32),
            pltpu.VMEM((6, PLANES, ROWS, BY), f32),
            pltpu.VMEM((5, PLANES, ROWS, BY), f32),
            pltpu.VMEM((2, BX // 2, BZ, BY), f32),
            pltpu.VMEM((2, BX // 2, BZ, BY), f32),
            pltpu.VMEM((3, PLANES + 2) + plane, f32),
            pltpu.VMEM((PLANES,) + plane, f32),
            pltpu.VMEM((PLANES,) + plane, f32),
            pltpu.VMEM((PLANES,) + plane, f32),
            pltpu.VMEM((PLANES,) + plane, f32),
            pltpu.VMEM((PLANES, BZ, BY), f32),
            pltpu.VMEM((3, BZ, BY), f32),
            pltpu.VMEM((partners, BZ, BY), f32),
            dma((5,)), dma((2,)), dma((2,)),
            dma((8,)), dma((8,)), dma((8,)), dma((8,)), dma((8,)), dma((8,)),
            dma((3,)), dma((3,)),
        ],
        name="stokes",
        compiler_params=pltpu.CompilerParams(
            collective_id=0, has_side_effects=True, vmem_limit_bytes=32 * 1024 * 1024),
    )(vel_x, vel_y, vel_z, pressure, phase, visc_scale, power_n, density)
    return pl.pallas_call(
        split_kernel,
        out_shape=[jax.ShapeDtypeStruct((BX, BZ, BY), f32)] * 5,
        in_specs=[vmem],
        out_specs=[vmem] * 5,
        name="split",
    )(stacked)


def solution(mesh, z_lo=Z_LO):
    sizes = (mesh.shape["gx"], mesh.shape["gy"], mesh.shape["gz"], z_lo)
    block = P("gx", "gz", "gy")
    return jax.shard_map(
        functools.partial(local, sizes),
        mesh=mesh,
        in_specs=(block,) * 5 + (P(),) * 3,
        out_specs=(block,) * 5,
        check_vma=False,
    )
```

```python
import functools
import itertools

import jax
import jax.numpy as jnp
from jax import lax
from jax.experimental import pallas as pl
from jax.experimental.pallas import tpu as pltpu
from jax.sharding import PartitionSpec as P

ITERS = 4
PHASES = 4
STRAIN_FLOOR = 1.0
PRESSURE_STEP = 0.5
VELOCITY_STEP = 0.1

BX, BZ, BY = 16, 8, 128
LOW, HIGH = 2, 4
YLOW, YHIGH = 4, 8
PLANES = BX + LOW + HIGH
ROWS = 2 * BZ
GROUP = YLOW + YHIGH
Z_LO = 4
VMEM_BYTES = 62 * 1024 * 1024
MESH = pl.DeviceIdType.MESH

SIDES = tuple((a, b) for a in (-1, 0, 1) for b in (-1, 0, 1) if (a, b) != (0, 0))


def send_planes(a):
    return {0: (LOW, BX), 1: (LOW + BX - LOW, LOW), -1: (LOW, HIGH)}[a]


def land_planes(a):
    return {0: LOW, 1: 0, -1: LOW + BX}[a]


def send_rows(b):
    return {0: (0, BZ), 1: (BZ - LOW, LOW), -1: (0, HIGH)}[b]


def land_rows(b):
    return {0: 0, 1: ROWS - LOW, -1: BZ}[b]


def loop(lower, upper, body, carry, unroll):
    assert (upper - lower) % unroll == 0

    def several(n, c):
        for u in range(unroll):
            c = body(lower + n * unroll + u, c)
        return c

    return lax.fori_loop(0, (upper - lower) // unroll, several, carry)


def y_roll(x, s):
    r = pltpu.roll(x, s % BY, 1)
    swapped = jnp.concatenate([r[ROWS:], r[:ROWS]], axis=0)
    lane = lax.broadcasted_iota(jnp.int32, x.shape, 1)
    return jnp.where(lane == (0 if s == 1 else BY - 1), swapped, r)


def z_roll(x, s):
    return jnp.concatenate(
        [pltpu.roll(x[:ROWS], s % ROWS, 0), pltpu.roll(x[ROWS:], s % ROWS, 0)], axis=0
    )


def viscosity(rx, rz, ry, prefactor, power):
    div = rx + ry + rz
    third = div * (1.0 / 3.0)
    dx, dy, dz = rx - third, ry - third, rz - third
    inv = 0.5 * (dx * dx + dy * dy + dz * dz) + STRAIN_FLOOR
    return prefactor * jnp.exp(power * jnp.log(inv)), div


def kernel(sizes, vx_ref, vy_ref, vz_ref, p_ref, ph_ref, vs_in, pn_in, dn_in, out_ref,
           vs_ref, pn_ref, dn_ref, ph_in, first, second, s_pack, r_pack, vel, pres, pref, expo, rho, ar_src, ar_buf,
           in_sem, ysend, yrecv, send_a, recv_a, send_b, recv_b, send_c, recv_c, ar_send, ar_recv):
    ngx, ngy, ngz, z_lo = sizes
    gx, gy, gz = lax.axis_index("gx"), lax.axis_index("gy"), lax.axis_index("gz")

    in_copies = []
    for n, (src, dst) in enumerate(
        ((vx_ref, first.at[0, pl.ds(LOW, BX), pl.ds(0, BZ)]),
         (vz_ref, first.at[1, pl.ds(LOW, BX), pl.ds(0, BZ)]),
         (vy_ref, first.at[2, pl.ds(LOW, BX), pl.ds(0, BZ)]),
         (p_ref, first.at[3, pl.ds(LOW, BX), pl.ds(0, BZ)]),
         (ph_ref, ph_in), (vs_in, vs_ref), (pn_in, pn_ref), (dn_in, dn_ref))):
        cp = pltpu.make_async_copy(src, dst, in_sem.at[n])
        cp.start()
        in_copies.append(cp)

    n_x, n_y, n_z = ngx // z_lo, ngz // 2, z_lo * ngy

    def neighbour(a, b, c):
        return (lax.rem(gx + (a + ngx), ngx), lax.rem(gy + (c + ngy), ngy), lax.rem(gz + (b + ngz), ngz))

    chip_x, chip_y, core = gx // z_lo, gz // 2, lax.rem(gz, 2)
    chip_z = gy * z_lo + lax.rem(gx, z_lo)

    def far(x, y, z, c):
        z = lax.rem(chip_z + z, n_z)
        return (lax.rem(chip_x + x, n_x) * z_lo + lax.rem(z, z_lo), z // z_lo,
                lax.rem(chip_y + y, n_y) * 2 + lax.rem(core + c, 2))

    def hops(o):
        return sum(min(d, n - d) for d, n in zip(o, (n_x, n_y, n_z, 2)))

    def group(*counts):
        offsets = [o for o in itertools.product(*[range(n) for n in counts]) if any(o)]
        return [far(*o) for o in sorted(offsets, key=hops, reverse=True)]

    sum_phases = (group(1, 1, n_z, 2), group(n_x, n_y, 1, 1))

    barrier = pltpu.get_barrier_semaphore()
    greeted = [d for devices in sum_phases for d in devices]
    greeted += [neighbour(a, b, 0) for a, b in SIDES] + [neighbour(0, 0, -1), neighbour(0, 0, 1)]
    for d in greeted:
        pl.semaphore_signal(barrier, inc=1, device_id=d, device_id_type=MESH)

    lane_v = lax.broadcasted_iota(jnp.int32, (BZ, BY), 1)
    for cp in in_copies:
        cp.wait()
    first[4, LOW:LOW + BX, 0:BZ] = ph_in[...].astype(jnp.float32)

    def pack(k, carry):
        lo = jnp.zeros((BZ, BY), jnp.float32)
        hi = jnp.zeros((BZ, BY), jnp.float32)
        for q in range(2):
            for a in range(5):
                base = GROUP * a + 64 * q
                rolled = first[a, LOW + 2 * k + q, 0:BZ]
                if base:
                    rolled = pltpu.roll(rolled, base, 1)
                lo = jnp.where((lane_v >= base) & (lane_v < base + YHIGH), rolled, lo)
                if base:
                    hi = jnp.where((lane_v >= base - YLOW) & (lane_v < base), rolled, hi)
                else:
                    hi = jnp.where(lane_v >= BY - YLOW, rolled, hi)
        s_pack[0, k] = lo
        s_pack[1, k] = hi
        return carry

    loop(0, BX // 2, pack, 0, 4)
    pl.semaphore_wait(barrier, len(greeted))

    y_copies = []
    for n, c in enumerate((-1, 1)):
        cp = pltpu.make_async_remote_copy(
            src_ref=s_pack.at[n], dst_ref=r_pack.at[n], send_sem=ysend.at[n], recv_sem=yrecv.at[n],
            device_id=neighbour(0, 0, c), device_id_type=MESH)
        cp.start()
        y_copies.append(cp)

    def exchange(buf, lo, count, send, recv):
        copies = []
        for n, (a, b) in enumerate(SIDES):
            (p0, pn), (r0, rn) = send_planes(a), send_rows(b)
            cp = pltpu.make_async_remote_copy(
                src_ref=buf.at[pl.ds(lo, count), pl.ds(p0, pn), pl.ds(r0, rn)],
                dst_ref=buf.at[pl.ds(lo, count), pl.ds(land_planes(a), pn), pl.ds(land_rows(b), rn)],
                send_sem=send.at[n], recv_sem=recv.at[n],
                device_id=neighbour(a, b, 0), device_id_type=MESH)
            cp.start()
            copies.append(cp)
        return copies

    main_copies = exchange(first, 0, 5, send_a, recv_a)
    for cp in y_copies:
        cp.wait_recv()

    def unpack_y(k, carry):
        low_lane = lax.rem(lane_v + YLOW, 64)
        from_low = lax.rem(low_lane, GROUP) < YLOW
        both = jnp.where(from_low, r_pack[1, k], r_pack[0, k])
        first[5, LOW + 2 * k, 0:BZ] = both
        first[5, LOW + 2 * k + 1, 0:BZ] = pltpu.roll(both, 64, 1)
        return carry

    loop(0, BX // 2, unpack_y, 0, 8)
    halo_copies = exchange(first, 5, 1, send_b, recv_b)
    for cp in main_copies + halo_copies:
        cp.wait_recv()

    full = (2 * ROWS, BY)
    row = lax.broadcasted_iota(jnp.int32, full, 0)
    lane = lax.broadcasted_iota(jnp.int32, full, 1)
    half = row // ROWS
    zr = row - half * ROWS
    zi = gz * BZ + jnp.where(zr >= ROWS - LOW, zr - ROWS, zr)
    yi = gy * BY + jnp.where(half == 0, lane, jnp.where(lane >= BY // 2, lane - BY, lane + BY))
    in_zy = (zi >= 0) & (zi < ngz * BZ) & (yi >= 0) & (yi < ngy * BY)
    in_z1 = in_zy & (zi >= 1)
    in_y1 = in_zy & (yi >= 1)

    def x_of(j):
        return gx * BX - LOW + j

    def inside(j, comp):
        xi = x_of(j)
        high = xi < ngx * BX
        if comp == 0:
            return in_zy & ((xi >= 1) & high)
        return {1: in_z1, 2: in_y1, None: in_zy}[comp] & ((xi >= 0) & high)

    def whole(buf, count, a, j):
        packed = buf[count, j]
        halo = pltpu.roll(packed, BY - GROUP * a, 1) if a else packed
        return jnp.concatenate([buf[a, j], halo], axis=0)

    def lookup_rows(ref):
        return [jnp.full(full, ref[k], jnp.float32) for k in range(PHASES)]

    scales, powers, densities = lookup_rows(vs_ref), lookup_rows(pn_ref), lookup_rows(dn_ref)
    powers = [0.5 * (1.0 / n - 1.0) for n in powers]

    def select(phase, table):
        out = table[PHASES - 1]
        for k in range(PHASES - 2, -1, -1):
            out = jnp.where(phase == float(k), table[k], out)
        return out

    def unpack_first(j, carry):
        for a in range(3):
            vel[a, j + 1] = jnp.where(inside(j, a), whole(first, 5, a, j), 0.0)
        pres[j] = whole(first, 5, 3, j)
        phase = whole(first, 5, 4, j)
        pref[j] = jnp.where(inside(j, None), select(phase, scales), 0.0)
        expo[j] = select(phase, powers)
        rho[j] = select(phase, densities)
        return carry

    loop(0, PLANES, unpack_first, 0, 11)

    def iteration(first_plane, last_plane):
        zero = jnp.zeros(full, jnp.float32)

        def stage(j, carry):
            eta_m, tx_m, vz_m, vy_m, fzx_m, fyx_m, pz_m, py_m, az_m, ay_m, rho_m = carry
            vx, vz, vy = vel[0, j + 1], vel[1, j + 1], vel[2, j + 1]
            rx = vel[0, j + 2] - vx
            rz = z_roll(vz, -1) - vz
            ry = y_roll(vy, -1) - vy
            eta, div = viscosity(rx, rz, ry, pref[j], expo[j])
            p = pres[j] - PRESSURE_STEP * eta * div
            pres[j] = p
            tx, tz, ty = eta * rx - p, eta * rz - p, eta * ry - p
            ax = eta + eta_m
            az = eta + z_roll(eta, 1)
            ay = eta + y_roll(eta, 1)
            exz = ax + z_roll(ax, 1)
            exy = ax + y_roll(ax, 1)
            eyz = ay + z_roll(ay, 1)
            fzx = exz * (vz - vz_m)
            fyx = exy * (vy - vy_m)
            fxz = exz * (vx - z_roll(vx, 1))
            fxy = exy * (vx - y_roll(vx, 1))
            fyz = eyz * (vy - z_roll(vy, 1))
            fzy = eyz * (vz - y_roll(vz, 1))
            res = tx - tx_m + 0.25 * ((z_roll(fxz, -1) - fxz) + (y_roll(fxy, -1) - fxy))
            vel[0, j + 1] = jnp.where(inside(j, 0), vx + (2.0 * VELOCITY_STEP) * res / ax, 0.0)
            res = pz_m + 0.25 * (fzx - fzx_m) - rho_m
            vel[1, j] = jnp.where(inside(j - 1, 1), vz_m + (2.0 * VELOCITY_STEP) * res / az_m, 0.0)
            res = py_m + 0.25 * (fyx - fyx_m)
            vel[2, j] = jnp.where(inside(j - 1, 2), vy_m + (2.0 * VELOCITY_STEP) * res / ay_m, 0.0)
            pz = tz - z_roll(tz, 1) + 0.25 * (y_roll(fzy, -1) - fzy)
            py = ty - y_roll(ty, 1) + 0.25 * (z_roll(fyz, -1) - fyz)
            return eta, tx, vz, vy, fzx, fyx, pz, py, az, ay, rho[j]

        loop(first_plane, last_plane + 1, stage, (zero,) * 11, (last_plane + 1 - first_plane) // 3)

    iteration(0, PLANES - 2)
    iteration(1, PLANES - HIGH)

    own = lax.broadcasted_iota(jnp.int32, (BZ, BY), 1)

    def repack(i, carry):
        packed = jnp.zeros((BZ, BY), jnp.float32)
        for a in range(4):
            block = vel[a, i + LOW + 1] if a < 3 else pres[i + LOW]
            second[a, i + LOW, 0:BZ] = block[0:BZ]
            halo = block[ROWS:ROWS + BZ]
            base = GROUP * a
            if base:
                halo = pltpu.roll(halo, base, 1)
                packed = jnp.where((own >= base - YLOW) & (own < base + YHIGH), halo, packed)
            else:
                packed = halo
        second[4, i + LOW, 0:BZ] = packed
        return carry

    loop(0, BX, repack, 0, 8)
    second_copies = exchange(second, 0, 5, send_c, recv_c)
    for cp in second_copies:
        cp.wait_recv()

    def unpack_second(j, carry):
        for a in range(3):
            vel[a, j + 1] = jnp.where(inside(j, a), whole(second, 4, a, j), 0.0)
        pres[j] = whole(second, 4, 3, j)
        return carry

    loop(0, PLANES, unpack_second, 0, 11)
    iteration(0, PLANES - 2)

    lane_0 = lane_v == 0

    def last_pressure(i, total):
        j = i + LOW
        vx = vel[0, j + 1, 0:BZ]
        vz = vel[1, j + 1, 0:ROWS]
        vy = vel[2, j + 1, 0:BZ]
        rx = vel[0, j + 2, 0:BZ] - vx
        rz = (pltpu.roll(vz, ROWS - 1, 0) - vz)[0:BZ]
        next_y = jnp.where(lane_0, vel[2, j + 1, ROWS:ROWS + BZ], vy)
        ry = pltpu.roll(next_y, BY - 1, 1) - vy
        eta, div = viscosity(rx, rz, ry, pref[j, 0:BZ], expo[j, 0:BZ])
        p = pres[j, 0:BZ] - PRESSURE_STEP * eta * div
        out_ref[3, i] = p
        out_ref[4, i] = eta
        return total + p

    total = loop(0, BX, last_pressure, jnp.zeros((BZ, BY), jnp.float32), 8)

    base = 0
    sum_sends = []
    for n, devices in enumerate(sum_phases):
        count = len(devices)
        ar_src[n] = total
        for o, d in enumerate(devices):
            pltpu.make_async_remote_copy(
                src_ref=ar_src.at[n], dst_ref=ar_buf.at[base + o], send_sem=ar_send.at[n], recv_sem=ar_recv.at[n],
                device_id=d, device_id_type=MESH).start()
        part = ar_buf.at[pl.ds(base, count)]
        sum_sends.append(pltpu.make_async_copy(part, part, ar_send.at[n]))
        if n == 0:
            iteration(1, PLANES - HIGH)
            out_ref[0] = vel[0, LOW + 1:LOW + 1 + BX, 0:BZ]
            out_ref[1] = vel[2, LOW + 1:LOW + 1 + BX, 0:BZ]
            out_ref[2] = vel[1, LOW + 1:LOW + 1 + BX, 0:BZ]
        pltpu.make_async_copy(part, part, ar_recv.at[n]).wait()
        for o in range(count):
            total = total + ar_buf[base + o]
        base += count
    cells = float(ngx * ngy * ngz * BX * BZ * BY)
    mean = jnp.sum(total) / cells
    out_ref[3] = out_ref[3] - mean

    for cp in y_copies + main_copies + halo_copies + second_copies:
        cp.wait_send()
    for cp in sum_sends:
        cp.wait()


def split_kernel(in_ref, *refs):
    *outs, sem = refs
    copies = [pltpu.make_async_copy(in_ref.at[n], out, sem.at[n]) for n, out in enumerate(outs)]
    for cp in copies:
        cp.start()
    for cp in copies:
        cp.wait()


def local(sizes, vel_x, vel_y, vel_z, pressure, phase, visc_scale, power_n, density):
    ngx, ngy, ngz, z_lo = sizes
    partners = (z_lo * ngy * 2 - 1) + (ngx // z_lo * (ngz // 2) - 1)
    f32 = jnp.float32
    hbm = pl.BlockSpec(memory_space=pltpu.HBM)
    vmem = pl.BlockSpec(memory_space=pltpu.VMEM)
    dma = pltpu.SemaphoreType.DMA
    plane = (2 * ROWS, BY)
    stacked = pl.pallas_call(
        functools.partial(kernel, sizes),
        out_shape=jax.ShapeDtypeStruct((5, BX, BZ, BY), f32),
        in_specs=[hbm] * 8,
        out_specs=vmem,
        scratch_shapes=[
            pltpu.SMEM((PHASES,), f32),
            pltpu.SMEM((PHASES,), f32),
            pltpu.SMEM((PHASES,), f32),
            pltpu.VMEM((BX, BZ, BY), jnp.int32),
            pltpu.VMEM((6, PLANES, ROWS, BY), f32),
            pltpu.VMEM((5, PLANES, ROWS, BY), f32),
            pltpu.VMEM((2, BX // 2, BZ, BY), f32),
            pltpu.VMEM((2, BX // 2, BZ, BY), f32),
            pltpu.VMEM((3, PLANES + 2) + plane, f32),
            pltpu.VMEM((PLANES,) + plane, f32),
            pltpu.VMEM((PLANES,) + plane, f32),
            pltpu.VMEM((PLANES,) + plane, f32),
            pltpu.VMEM((PLANES,) + plane, f32),
            pltpu.VMEM((2, BZ, BY), f32),
            pltpu.VMEM((partners, BZ, BY), f32),
            dma((8,)), dma((2,)), dma((2,)),
            dma((8,)), dma((8,)), dma((8,)), dma((8,)), dma((8,)), dma((8,)),
            dma((2,)), dma((2,)),
        ],
        name="stokes",
        compiler_params=pltpu.CompilerParams(
            collective_id=0, has_side_effects=True, vmem_limit_bytes=VMEM_BYTES),
    )(vel_x, vel_y, vel_z, pressure, phase, visc_scale, power_n, density)
    return pl.pallas_call(
        split_kernel,
        out_shape=[jax.ShapeDtypeStruct((BX, BZ, BY), f32)] * 5,
        in_specs=[hbm],
        out_specs=[hbm] * 5,
        scratch_shapes=[dma((5,))],
        name="split",
        compiler_params=pltpu.CompilerParams(vmem_limit_bytes=VMEM_BYTES),
    )(stacked)


def solution(mesh, z_lo=Z_LO):
    sizes = (mesh.shape["gx"], mesh.shape["gy"], mesh.shape["gz"], z_lo)
    block = P("gx", "gz", "gy")
    return jax.shard_map(
        functools.partial(local, sizes),
        mesh=mesh,
        in_specs=(block,) * 5 + (P(),) * 3,
        out_specs=(block,) * 5,
        check_vma=False,
    )
```

```python
import functools
import itertools

import jax
import jax.numpy as jnp
from jax import lax
from jax.experimental import pallas as pl
from jax.experimental.pallas import tpu as pltpu
from jax.sharding import PartitionSpec as P

ITERS = 4
PHASES = 4
STRAIN_FLOOR = 1.0
PRESSURE_STEP = 0.5
VELOCITY_STEP = 0.1

BX, BZ, BY = 16, 8, 128
LOW, HIGH = 2, 4
YLOW, YHIGH = 4, 8
PLANES = BX + LOW + HIGH
ROWS = 2 * BZ
GROUP = YLOW + YHIGH
Z_LO = 4
VMEM_BYTES = 62 * 1024 * 1024
MESH = pl.DeviceIdType.MESH

SIDES = tuple((a, b) for a in (-1, 0, 1) for b in (-1, 0, 1) if (a, b) != (0, 0))


def send_planes(a):
    return {0: (LOW, BX), 1: (LOW + BX - LOW, LOW), -1: (LOW, HIGH)}[a]


def land_planes(a):
    return {0: LOW, 1: 0, -1: LOW + BX}[a]


def send_rows(b):
    return {0: (0, BZ), 1: (BZ - LOW, LOW), -1: (0, HIGH)}[b]


def land_rows(b):
    return {0: 0, 1: ROWS - LOW, -1: BZ}[b]


def loop(lower, upper, body, carry, unroll):
    assert (upper - lower) % unroll == 0

    def several(n, c):
        for u in range(unroll):
            c = body(lower + n * unroll + u, c)
        return c

    return lax.fori_loop(0, (upper - lower) // unroll, several, carry)


def y_roll(x, s):
    r = pltpu.roll(x, s % BY, 1)
    swapped = jnp.concatenate([r[ROWS:], r[:ROWS]], axis=0)
    lane = lax.broadcasted_iota(jnp.int32, x.shape, 1)
    return jnp.where(lane == (0 if s == 1 else BY - 1), swapped, r)


def z_roll(x, s):
    return jnp.concatenate(
        [pltpu.roll(x[:ROWS], s % ROWS, 0), pltpu.roll(x[ROWS:], s % ROWS, 0)], axis=0
    )


def viscosity(rx, rz, ry, prefactor, power):
    div = rx + ry + rz
    third = div * (1.0 / 3.0)
    dx, dy, dz = rx - third, ry - third, rz - third
    inv = 0.5 * (dx * dx + dy * dy + dz * dz) + STRAIN_FLOOR
    return prefactor * jnp.exp(power * jnp.log(inv)), div


def kernel(sizes, vx_ref, vy_ref, vz_ref, p_ref, ph_ref, vs_in, pn_in, dn_in, out_ref,
           vs_ref, pn_ref, dn_ref, ph_in, first, second, s_pack, r_pack, vel, pres, pref, expo, rho, last_p, last_eta, ar_src, ar_buf,
           in_sem, ysend, yrecv, send_a, recv_a, send_b, recv_b, send_c, recv_c, ar_send, ar_recv, out_sem, here):
    ngx, ngy, ngz, z_lo = sizes
    gx, gy, gz = lax.axis_index("gx"), lax.axis_index("gy"), lax.axis_index("gz")

    in_copies = []
    for n, (src, dst) in enumerate(
        ((vx_ref, first.at[0, pl.ds(LOW, BX), pl.ds(0, BZ)]),
         (vz_ref, first.at[1, pl.ds(LOW, BX), pl.ds(0, BZ)]),
         (vy_ref, first.at[2, pl.ds(LOW, BX), pl.ds(0, BZ)]),
         (p_ref, first.at[3, pl.ds(LOW, BX), pl.ds(0, BZ)]),
         (ph_ref, ph_in), (vs_in, vs_ref), (pn_in, pn_ref), (dn_in, dn_ref))):
        cp = pltpu.make_async_copy(src, dst, in_sem.at[n])
        cp.start()
        in_copies.append(cp)

    n_x, n_y, n_z = ngx // z_lo, ngz // 2, z_lo * ngy

    def neighbour(a, b, c):
        return (lax.rem(gx + (a + ngx), ngx), lax.rem(gy + (c + ngy), ngy), lax.rem(gz + (b + ngz), ngz))

    chip_x, chip_y, core = gx // z_lo, gz // 2, lax.rem(gz, 2)
    chip_z = gy * z_lo + lax.rem(gx, z_lo)

    def far(x, y, z, c):
        z = lax.rem(chip_z + z, n_z)
        return (lax.rem(chip_x + x, n_x) * z_lo + lax.rem(z, z_lo), z // z_lo,
                lax.rem(chip_y + y, n_y) * 2 + lax.rem(core + c, 2))

    def hops(o):
        return sum(min(d, n - d) for d, n in zip(o, (n_x, n_y, n_z, 2)))

    def group(*counts):
        offsets = [o for o in itertools.product(*[range(n) for n in counts]) if any(o)]
        return [far(*o) for o in sorted(offsets, key=hops, reverse=True)]

    sum_phases = (group(1, 1, n_z, 2), group(n_x, n_y, 1, 1))

    barrier = pltpu.get_barrier_semaphore()
    greeted = [neighbour(0, 0, -1), neighbour(0, 0, 1)] + [neighbour(a, b, 0) for a, b in SIDES]
    for d in greeted:
        pl.semaphore_signal(barrier, inc=1, device_id=d, device_id_type=MESH)

    lane_v = lax.broadcasted_iota(jnp.int32, (BZ, BY), 1)
    for cp in in_copies:
        cp.wait()
    first[4, LOW:LOW + BX, 0:BZ] = ph_in[...].astype(jnp.float32)

    def pack(k, carry):
        lo = jnp.zeros((BZ, BY), jnp.float32)
        hi = jnp.zeros((BZ, BY), jnp.float32)
        for q in range(2):
            for a in range(5):
                base = GROUP * a + 64 * q
                rolled = first[a, LOW + 2 * k + q, 0:BZ]
                if base:
                    rolled = pltpu.roll(rolled, base, 1)
                lo = jnp.where((lane_v >= base) & (lane_v < base + YHIGH), rolled, lo)
                if base:
                    hi = jnp.where((lane_v >= base - YLOW) & (lane_v < base), rolled, hi)
                else:
                    hi = jnp.where(lane_v >= BY - YLOW, rolled, hi)
        s_pack[0, k] = lo
        s_pack[1, k] = hi
        return carry

    loop(0, BX // 2, pack, 0, 4)
    pl.semaphore_wait(barrier, len(greeted))

    y_copies = []
    for n, c in enumerate((-1, 1)):
        cp = pltpu.make_async_remote_copy(
            src_ref=s_pack.at[n], dst_ref=r_pack.at[n], send_sem=ysend.at[n], recv_sem=yrecv.at[n],
            device_id=neighbour(0, 0, c), device_id_type=MESH)
        cp.start()
        y_copies.append(cp)

    def exchange(buf, lo, count, send, recv):
        copies = []
        for n, (a, b) in enumerate(SIDES):
            (p0, pn), (r0, rn) = send_planes(a), send_rows(b)
            cp = pltpu.make_async_remote_copy(
                src_ref=buf.at[pl.ds(lo, count), pl.ds(p0, pn), pl.ds(r0, rn)],
                dst_ref=buf.at[pl.ds(lo, count), pl.ds(land_planes(a), pn), pl.ds(land_rows(b), rn)],
                send_sem=send.at[n], recv_sem=recv.at[n],
                device_id=neighbour(a, b, 0), device_id_type=MESH)
            cp.start()
            copies.append(cp)
        return copies

    main_copies = exchange(first, 0, 5, send_a, recv_a)
    for cp in y_copies:
        cp.wait_recv()

    def unpack_y(k, carry):
        low_lane = lax.rem(lane_v + YLOW, 64)
        from_low = lax.rem(low_lane, GROUP) < YLOW
        both = jnp.where(from_low, r_pack[1, k], r_pack[0, k])
        first[5, LOW + 2 * k, 0:BZ] = both
        first[5, LOW + 2 * k + 1, 0:BZ] = pltpu.roll(both, 64, 1)
        return carry

    loop(0, BX // 2, unpack_y, 0, 8)
    halo_copies = exchange(first, 5, 1, send_b, recv_b)
    for cp in main_copies + halo_copies:
        cp.wait_recv()

    full = (2 * ROWS, BY)
    row = lax.broadcasted_iota(jnp.int32, full, 0)
    lane = lax.broadcasted_iota(jnp.int32, full, 1)
    half = row // ROWS
    zr = row - half * ROWS
    zi = gz * BZ + jnp.where(zr >= ROWS - LOW, zr - ROWS, zr)
    yi = gy * BY + jnp.where(half == 0, lane, jnp.where(lane >= BY // 2, lane - BY, lane + BY))
    in_zy = (zi >= 0) & (zi < ngz * BZ) & (yi >= 0) & (yi < ngy * BY)
    in_z1 = in_zy & (zi >= 1)
    in_y1 = in_zy & (yi >= 1)

    def x_of(j):
        return gx * BX - LOW + j

    def inside(j, comp):
        xi = x_of(j)
        high = xi < ngx * BX
        if comp == 0:
            return in_zy & ((xi >= 1) & high)
        return {1: in_z1, 2: in_y1, None: in_zy}[comp] & ((xi >= 0) & high)

    def whole(buf, count, a, j):
        packed = buf[count, j]
        halo = pltpu.roll(packed, BY - GROUP * a, 1) if a else packed
        return jnp.concatenate([buf[a, j], halo], axis=0)

    def lookup_rows(ref):
        return [jnp.full(full, ref[k], jnp.float32) for k in range(PHASES)]

    scales, powers, densities = lookup_rows(vs_ref), lookup_rows(pn_ref), lookup_rows(dn_ref)
    powers = [0.5 * (1.0 / n - 1.0) for n in powers]

    def select(phase, table):
        out = table[PHASES - 1]
        for k in range(PHASES - 2, -1, -1):
            out = jnp.where(phase == float(k), table[k], out)
        return out

    def unpack_first(j, carry):
        for a in range(3):
            vel[a, j + 1] = jnp.where(inside(j, a), whole(first, 5, a, j), 0.0)
        pres[j] = whole(first, 5, 3, j)
        phase = whole(first, 5, 4, j)
        pref[j] = jnp.where(inside(j, None), select(phase, scales), 0.0)
        expo[j] = select(phase, powers)
        rho[j] = select(phase, densities)
        return carry

    loop(0, PLANES, unpack_first, 0, 11)

    def iteration(first_plane, last_plane):
        zero = jnp.zeros(full, jnp.float32)

        def stage(j, carry):
            eta_m, tx_m, vz_m, vy_m, fzx_m, fyx_m, pz_m, py_m, az_m, ay_m, rho_m = carry
            vx, vz, vy = vel[0, j + 1], vel[1, j + 1], vel[2, j + 1]
            rx = vel[0, j + 2] - vx
            rz = z_roll(vz, -1) - vz
            ry = y_roll(vy, -1) - vy
            eta, div = viscosity(rx, rz, ry, pref[j], expo[j])
            p = pres[j] - PRESSURE_STEP * eta * div
            pres[j] = p
            tx, tz, ty = eta * rx - p, eta * rz - p, eta * ry - p
            ax = eta + eta_m
            az = eta + z_roll(eta, 1)
            ay = eta + y_roll(eta, 1)
            exz = ax + z_roll(ax, 1)
            exy = ax + y_roll(ax, 1)
            eyz = ay + z_roll(ay, 1)
            fzx = exz * (vz - vz_m)
            fyx = exy * (vy - vy_m)
            fxz = exz * (vx - z_roll(vx, 1))
            fxy = exy * (vx - y_roll(vx, 1))
            fyz = eyz * (vy - z_roll(vy, 1))
            fzy = eyz * (vz - y_roll(vz, 1))
            res = tx - tx_m + 0.25 * ((z_roll(fxz, -1) - fxz) + (y_roll(fxy, -1) - fxy))
            vel[0, j + 1] = jnp.where(inside(j, 0), vx + (2.0 * VELOCITY_STEP) * res / ax, 0.0)
            res = pz_m + 0.25 * (fzx - fzx_m) - rho_m
            vel[1, j] = jnp.where(inside(j - 1, 1), vz_m + (2.0 * VELOCITY_STEP) * res / az_m, 0.0)
            res = py_m + 0.25 * (fyx - fyx_m)
            vel[2, j] = jnp.where(inside(j - 1, 2), vy_m + (2.0 * VELOCITY_STEP) * res / ay_m, 0.0)
            pz = tz - z_roll(tz, 1) + 0.25 * (y_roll(fzy, -1) - fzy)
            py = ty - y_roll(ty, 1) + 0.25 * (z_roll(fyz, -1) - fyz)
            return eta, tx, vz, vy, fzx, fyx, pz, py, az, ay, rho[j]

        loop(first_plane, last_plane + 1, stage, (zero,) * 11, (last_plane + 1 - first_plane) // 3)

    iteration(0, PLANES - 2)
    iteration(1, PLANES - HIGH)

    own = lax.broadcasted_iota(jnp.int32, (BZ, BY), 1)

    def repack(i, carry):
        packed = jnp.zeros((BZ, BY), jnp.float32)
        for a in range(4):
            block = vel[a, i + LOW + 1] if a < 3 else pres[i + LOW]
            second[a, i + LOW, 0:BZ] = block[0:BZ]
            halo = block[ROWS:ROWS + BZ]
            base = GROUP * a
            if base:
                halo = pltpu.roll(halo, base, 1)
                packed = jnp.where((own >= base - YLOW) & (own < base + YHIGH), halo, packed)
            else:
                packed = halo
        second[4, i + LOW, 0:BZ] = packed
        return carry

    loop(0, BX, repack, 0, 8)
    second_copies = exchange(second, 0, 5, send_c, recv_c)
    for a, b in SIDES:
        pl.semaphore_signal(here.at[0], inc=1, device_id=neighbour(2 * a, 2 * b, 0), device_id_type=MESH)
    for cp in second_copies:
        cp.wait_recv()

    def unpack_second(j, carry):
        for a in range(3):
            vel[a, j + 1] = jnp.where(inside(j, a), whole(second, 4, a, j), 0.0)
        pres[j] = whole(second, 4, 3, j)
        return carry

    loop(0, PLANES, unpack_second, 0, 11)
    iteration(0, PLANES - 2)

    lane_0 = lane_v == 0

    def last_pressure(i, total):
        j = i + LOW
        vx = vel[0, j + 1, 0:BZ]
        vz = vel[1, j + 1, 0:ROWS]
        vy = vel[2, j + 1, 0:BZ]
        rx = vel[0, j + 2, 0:BZ] - vx
        rz = (pltpu.roll(vz, ROWS - 1, 0) - vz)[0:BZ]
        next_y = jnp.where(lane_0, vel[2, j + 1, ROWS:ROWS + BZ], vy)
        ry = pltpu.roll(next_y, BY - 1, 1) - vy
        eta, div = viscosity(rx, rz, ry, pref[j, 0:BZ], expo[j, 0:BZ])
        p = pres[j, 0:BZ] - PRESSURE_STEP * eta * div
        last_p[i] = p
        last_eta[i] = eta
        return total + p

    total = loop(0, BX, last_pressure, jnp.zeros((BZ, BY), jnp.float32), 8)

    total = jnp.sum(total, axis=0, keepdims=True)
    eta_copy = pltpu.make_async_copy(last_eta, out_ref.at[4], out_sem.at[4])
    eta_copy.start()
    out_copies = [eta_copy]
    base = 0
    sum_sends = []
    for n, devices in enumerate(sum_phases):
        count = len(devices)
        ar_src[n] = total
        pl.semaphore_wait(here.at[n], len(SIDES))
        for o, d in enumerate(devices):
            pltpu.make_async_remote_copy(
                src_ref=ar_src.at[n], dst_ref=ar_buf.at[base + o], send_sem=ar_send.at[n], recv_sem=ar_recv.at[n],
                device_id=d, device_id_type=MESH).start()
        part = ar_buf.at[pl.ds(base, count)]
        sum_sends.append(pltpu.make_async_copy(part, part, ar_send.at[n]))
        if n == 0:
            for a, b in SIDES:
                pl.semaphore_signal(here.at[1], inc=1, device_id=neighbour(4 * a, 4 * b, 0), device_id_type=MESH)
            iteration(1, PLANES - HIGH)
            for a, comp in enumerate((0, 2, 1)):
                out_v = vel.at[comp, pl.ds(LOW + 1, BX), pl.ds(0, BZ)]
                cp = pltpu.make_async_copy(out_v, out_ref.at[a], out_sem.at[a])
                cp.start()
                out_copies.append(cp)
        pltpu.make_async_copy(part, part, ar_recv.at[n]).wait()
        for o in range(count):
            total = total + ar_buf[base + o]
        base += count
    cells = float(ngx * ngy * ngz * BX * BZ * BY)
    mean = jnp.sum(total) / cells
    last_p[...] = last_p[...] - mean
    p_copy = pltpu.make_async_copy(last_p, out_ref.at[3], out_sem.at[3])
    p_copy.start()
    out_copies.append(p_copy)

    for cp in y_copies + main_copies + halo_copies + second_copies:
        cp.wait_send()
    for cp in sum_sends + out_copies:
        cp.wait()


def split_kernel(in_ref, *refs):
    *outs, held, sem_in, sem_out = refs
    into = [pltpu.make_async_copy(in_ref.at[n], held.at[n], sem_in.at[n]) for n in range(5)]
    back = [pltpu.make_async_copy(held.at[n], out, sem_out.at[n]) for n, out in enumerate(outs)]
    for cp in into:
        cp.start()
    for cp, after in zip(into, back):
        cp.wait()
        after.start()
    for cp in back:
        cp.wait()


def local(sizes, vel_x, vel_y, vel_z, pressure, phase, visc_scale, power_n, density):
    ngx, ngy, ngz, z_lo = sizes
    partners = (z_lo * ngy * 2 - 1) + (ngx // z_lo * (ngz // 2) - 1)
    f32 = jnp.float32
    hbm = pl.BlockSpec(memory_space=pltpu.HBM)
    dma = pltpu.SemaphoreType.DMA
    plane = (2 * ROWS, BY)
    stacked = pl.pallas_call(
        functools.partial(kernel, sizes),
        out_shape=jax.ShapeDtypeStruct((5, BX, BZ, BY), f32),
        in_specs=[hbm] * 8,
        out_specs=hbm,
        scratch_shapes=[
            pltpu.SMEM((PHASES,), f32),
            pltpu.SMEM((PHASES,), f32),
            pltpu.SMEM((PHASES,), f32),
            pltpu.VMEM((BX, BZ, BY), jnp.int32),
            pltpu.VMEM((6, PLANES, ROWS, BY), f32),
            pltpu.VMEM((5, PLANES, ROWS, BY), f32),
            pltpu.VMEM((2, BX // 2, BZ, BY), f32),
            pltpu.VMEM((2, BX // 2, BZ, BY), f32),
            pltpu.VMEM((3, PLANES + 2) + plane, f32),
            pltpu.VMEM((PLANES,) + plane, f32),
            pltpu.VMEM((PLANES,) + plane, f32),
            pltpu.VMEM((PLANES,) + plane, f32),
            pltpu.VMEM((PLANES,) + plane, f32),
            pltpu.VMEM((BX, BZ, BY), f32),
            pltpu.VMEM((BX, BZ, BY), f32),
            pltpu.VMEM((2, 1, BY), f32),
            pltpu.VMEM((partners, 1, BY), f32),
            dma((8,)), dma((2,)), dma((2,)),
            dma((8,)), dma((8,)), dma((8,)), dma((8,)), dma((8,)), dma((8,)),
            dma((2,)), dma((2,)), dma((5,)), pltpu.SemaphoreType.REGULAR((2,)),
        ],
        name="stokes",
        compiler_params=pltpu.CompilerParams(
            collective_id=0, has_side_effects=True, vmem_limit_bytes=VMEM_BYTES),
    )(vel_x, vel_y, vel_z, pressure, phase, visc_scale, power_n, density)
    return pl.pallas_call(
        split_kernel,
        out_shape=[jax.ShapeDtypeStruct((BX, BZ, BY), f32)] * 5,
        in_specs=[hbm],
        out_specs=[hbm] * 5,
        scratch_shapes=[pltpu.VMEM((5, BX, BZ, BY), f32), dma((5,)), dma((5,))],
        name="split",
        compiler_params=pltpu.CompilerParams(vmem_limit_bytes=VMEM_BYTES),
    )(stacked)


def solution(mesh, z_lo=Z_LO):
    sizes = (mesh.shape["gx"], mesh.shape["gy"], mesh.shape["gz"], z_lo)
    block = P("gx", "gz", "gy")
    return jax.shard_map(
        functools.partial(local, sizes),
        mesh=mesh,
        in_specs=(block,) * 5 + (P(),) * 3,
        out_specs=(block,) * 5,
        check_vma=False,
    )
```

```python
import functools
import itertools

import jax
import jax.numpy as jnp
from jax import lax
from jax.experimental import pallas as pl
from jax.experimental.pallas import tpu as pltpu
from jax.sharding import PartitionSpec as P

ITERS = 4
PHASES = 4
STRAIN_FLOOR = 1.0
PRESSURE_STEP = 0.5
VELOCITY_STEP = 0.1

BX, BZ, BY = 16, 8, 128
LOW, HIGH = 2, 4
YLOW, YHIGH = 4, 8
PLANES = BX + LOW + HIGH
ROWS = 2 * BZ
GROUP = YLOW + YHIGH
SHIFT = YHIGH + YLOW
LEFT_AT, LEFT = 118, 30
Z_LO = 4
VMEM_BYTES = 62 * 1024 * 1024
MESH = pl.DeviceIdType.MESH

SIDES = tuple((a, b) for a in (-1, 0, 1) for b in (-1, 0, 1) if (a, b) != (0, 0))


def send_planes(a):
    return {0: (LOW, BX), 1: (LOW + BX - LOW, LOW), -1: (LOW, HIGH)}[a]


def land_planes(a):
    return {0: LOW, 1: 0, -1: LOW + BX}[a]


def send_rows(b):
    return {0: (0, BZ), 1: (BZ - LOW, LOW), -1: (0, HIGH)}[b]


def land_rows(b):
    return {0: 0, 1: ROWS - LOW, -1: BZ}[b]


def loop(lower, upper, body, carry, unroll):
    assert (upper - lower) % unroll == 0

    def several(n, c):
        for u in range(unroll):
            c = body(lower + n * unroll + u, c)
        return c

    return lax.fori_loop(0, (upper - lower) // unroll, several, carry)


def y_roll(x, s):
    return pltpu.roll(x, s % BY, 1)


def z_roll(x, s):
    return pltpu.roll(x, s % ROWS, 0)


def viscosity(rx, rz, ry, prefactor, power):
    div = rx + ry + rz
    third = div * (1.0 / 3.0)
    dx, dy, dz = rx - third, ry - third, rz - third
    inv = 0.5 * (dx * dx + dy * dy + dz * dz) + STRAIN_FLOOR
    return prefactor * jnp.exp(power * jnp.log(inv)), div


def kernel(sizes, vx_ref, vy_ref, vz_ref, p_ref, ph_ref, vs_in, pn_in, dn_in, out_ref,
           vs_ref, pn_ref, dn_ref, ph_in, first, second, s_pack, r_pack, vel, pres, pref, expo, rho, last_v, last_p, last_eta, ar_src, ar_buf,
           in_sem, ysend, yrecv, send_a, recv_a, send_b, recv_b, send_c, recv_c, send_d, recv_d, ar_send, ar_recv, out_sem, here):
    ngx, ngy, ngz, z_lo = sizes
    gx, gy, gz = lax.axis_index("gx"), lax.axis_index("gy"), lax.axis_index("gz")

    n_x, n_y, n_z = ngx // z_lo, ngz // 2, z_lo * ngy

    def neighbour(a, b, c):
        return (lax.rem(gx + (a + ngx), ngx), lax.rem(gy + (c + ngy), ngy), lax.rem(gz + (b + ngz), ngz))

    chip_x, chip_y, core = gx // z_lo, gz // 2, lax.rem(gz, 2)
    chip_z = gy * z_lo + lax.rem(gx, z_lo)

    def far(x, y, z, c):
        z = lax.rem(chip_z + z, n_z)
        return (lax.rem(chip_x + x, n_x) * z_lo + lax.rem(z, z_lo), z // z_lo,
                lax.rem(chip_y + y, n_y) * 2 + lax.rem(core + c, 2))

    def hops(o):
        return sum(min(d, n - d) for d, n in zip(o, (n_x, n_y, n_z, 2)))

    def group(*counts):
        offsets = [o for o in itertools.product(*[range(n) for n in counts]) if any(o)]
        return [far(*o) for o in sorted(offsets, key=hops, reverse=True)]

    sum_phases = (group(1, 1, n_z, 2), group(n_x, n_y, 1, 1))

    barrier = pltpu.get_barrier_semaphore()
    greeted = [neighbour(0, 0, -1), neighbour(0, 0, 1)] + [neighbour(a, b, 0) for a, b in SIDES]
    for d in greeted:
        pl.semaphore_signal(barrier, inc=1, device_id=d, device_id_type=MESH)

    in_copies = []
    for n, (src, dst) in enumerate(
        ((vx_ref, first.at[0, pl.ds(LOW, BX), pl.ds(0, BZ)]),
         (vz_ref, first.at[1, pl.ds(LOW, BX), pl.ds(0, BZ)]),
         (vy_ref, first.at[2, pl.ds(LOW, BX), pl.ds(0, BZ)]),
         (p_ref, first.at[3, pl.ds(LOW, BX), pl.ds(0, BZ)]),
         (ph_ref, ph_in), (vs_in, vs_ref), (pn_in, pn_ref), (dn_in, dn_ref))):
        cp = pltpu.make_async_copy(src, dst, in_sem.at[n])
        cp.start()
        in_copies.append(cp)


    lane_v = lax.broadcasted_iota(jnp.int32, (BZ, BY), 1)
    for cp in in_copies:
        cp.wait()
    first[4, LOW:LOW + BX, 0:BZ] = ph_in[...].astype(jnp.float32)

    def pack(k, carry):
        lo = jnp.zeros((BZ, BY), jnp.float32)
        hi = jnp.zeros((BZ, BY), jnp.float32)
        for q in range(2):
            for a in range(5):
                base = GROUP * a + 64 * q
                rolled = first[a, LOW + 2 * k + q, 0:BZ]
                if base:
                    rolled = pltpu.roll(rolled, base, 1)
                lo = jnp.where((lane_v >= base) & (lane_v < base + YHIGH), rolled, lo)
                if base:
                    hi = jnp.where((lane_v >= base - YLOW) & (lane_v < base), rolled, hi)
                else:
                    hi = jnp.where(lane_v >= BY - YLOW, rolled, hi)
        s_pack[0, k] = lo
        s_pack[1, k] = hi
        return carry

    loop(0, BX // 2, pack, 0, 4)
    pl.semaphore_wait(barrier, len(greeted))

    y_copies = []
    for n, c in enumerate((-1, 1)):
        cp = pltpu.make_async_remote_copy(
            src_ref=s_pack.at[n], dst_ref=r_pack.at[n], send_sem=ysend.at[n], recv_sem=yrecv.at[n],
            device_id=neighbour(0, 0, c), device_id_type=MESH)
        cp.start()
        y_copies.append(cp)

    def exchange(buf, lo, count, send, recv):
        copies = []
        for n, (a, b) in enumerate(SIDES):
            (p0, pn), (r0, rn) = send_planes(a), send_rows(b)
            cp = pltpu.make_async_remote_copy(
                src_ref=buf.at[pl.ds(lo, count), pl.ds(p0, pn), pl.ds(r0, rn)],
                dst_ref=buf.at[pl.ds(lo, count), pl.ds(land_planes(a), pn), pl.ds(land_rows(b), rn)],
                send_sem=send.at[n], recv_sem=recv.at[n],
                device_id=neighbour(a, b, 0), device_id_type=MESH)
            cp.start()
            copies.append(cp)
        return copies

    main_copies = exchange(first, 0, 5, send_a, recv_a)
    for cp in y_copies:
        cp.wait_recv()

    def unpack_y(k, carry):
        low_lane = lax.rem(lane_v + YLOW, 64)
        from_low = lax.rem(low_lane, GROUP) < YLOW
        both = jnp.where(from_low, r_pack[1, k], r_pack[0, k])
        first[5, LOW + 2 * k, 0:BZ] = both
        first[5, LOW + 2 * k + 1, 0:BZ] = pltpu.roll(both, 64, 1)
        return carry

    loop(0, BX // 2, unpack_y, 0, 8)
    halo_copies = exchange(first, 5, 1, send_b, recv_b)

    full = (ROWS, BY)
    row = lax.broadcasted_iota(jnp.int32, full, 0)
    lane = lax.broadcasted_iota(jnp.int32, full, 1)
    zi = gz * BZ + jnp.where(row >= ROWS - LOW, row - ROWS, row)
    in_strip = jnp.where(lane < YHIGH, lane + BY, jnp.where(lane < BY // 2, lane - SHIFT, lane))
    in_z = (zi >= 0) & (zi < ngz * BZ)
    masks = []
    for cell in (lane, in_strip):
        yi = gy * BY + cell
        in_zy = in_z & (yi >= 0) & (yi < ngy * BY)
        masks.append({None: in_zy, 0: in_zy, 1: in_zy & (zi >= 1), 2: in_zy & (yi >= 1)})

    def inside(part, j, comp):
        xi = gx * BX - LOW + j
        return masks[part][comp] & ((xi >= (1 if comp == 0 else 0)) & (xi < ngx * BX))

    def splat(ref):
        return [jnp.full(full, ref[k], jnp.float32) for k in range(PHASES)]

    scales, powers, densities = splat(vs_ref), splat(pn_ref), splat(dn_ref)
    powers = [0.5 * (1.0 / n - 1.0) for n in powers]

    def select(phase, table):
        out = table[PHASES - 1]
        for k in range(PHASES - 2, -1, -1):
            out = jnp.where(phase == float(k), table[k], out)
        return out

    def unpack_first(part, j, whole):
        for a in range(3):
            vel[part, a, j + 1] = jnp.where(inside(part, j, a), whole(a, j), 0.0)
        pres[part, j] = whole(3, j)
        phase = whole(4, j)
        pref[part, j] = jnp.where(inside(part, j, None), select(phase, scales), 0.0)
        expo[part, j] = select(phase, powers)
        rho[part, j] = select(phase, densities)

    def unpack_second(part, j, whole):
        for a in range(3):
            vel[part, a, j + 1] = jnp.where(inside(part, j, a), whole(a, j), 0.0)
        pres[part, j] = whole(3, j)

    def strip_first(a, j):
        main = first[a, j]
        halo = first[5, j]
        if a:
            halo = pltpu.roll(halo, BY - GROUP * a, 1)
        low = pltpu.roll(jnp.where(lane >= BY - YLOW, halo, main), SHIFT, 1)
        return jnp.where(lane < YHIGH, halo, jnp.where(lane < BY // 2, low, main))

    def strip_second(a, j):
        packed = second[4, j]
        return pltpu.roll(packed, BY - LEFT * a, 1) if a else packed

    def unpack(function, part, whole):
        def body(j, carry):
            function(part, j, whole)
            return carry

        loop(0, PLANES, body, 0, 11)

    def iteration(part, first_plane, last_plane):
        zero = jnp.zeros(full, jnp.float32)

        def stage(j, carry):
            eta_m, tx_m, vz_m, vy_m, fzx_m, fyx_m, pz_m, py_m, az_m, ay_m, rho_m = carry
            vx, vz, vy = vel[part, 0, j + 1], vel[part, 1, j + 1], vel[part, 2, j + 1]
            rx = vel[part, 0, j + 2] - vx
            rz = z_roll(vz, -1) - vz
            ry = y_roll(vy, -1) - vy
            eta, div = viscosity(rx, rz, ry, pref[part, j], expo[part, j])
            p = pres[part, j] - PRESSURE_STEP * eta * div
            pres[part, j] = p
            tx, tz, ty = eta * rx - p, eta * rz - p, eta * ry - p
            ax = eta + eta_m
            az = eta + z_roll(eta, 1)
            ay = eta + y_roll(eta, 1)
            exz = ax + z_roll(ax, 1)
            exy = ax + y_roll(ax, 1)
            eyz = ay + z_roll(ay, 1)
            fzx = exz * (vz - vz_m)
            fyx = exy * (vy - vy_m)
            fxz = exz * (vx - z_roll(vx, 1))
            fxy = exy * (vx - y_roll(vx, 1))
            fyz = eyz * (vy - z_roll(vy, 1))
            fzy = eyz * (vz - y_roll(vz, 1))
            res = tx - tx_m + 0.25 * ((z_roll(fxz, -1) - fxz) + (y_roll(fxy, -1) - fxy))
            vel[part, 0, j + 1] = jnp.where(inside(part, j, 0), vx + (2.0 * VELOCITY_STEP) * res / ax, 0.0)
            res = pz_m + 0.25 * (fzx - fzx_m) - rho_m
            vel[part, 1, j] = jnp.where(inside(part, j - 1, 1), vz_m + (2.0 * VELOCITY_STEP) * res / az_m, 0.0)
            res = py_m + 0.25 * (fyx - fyx_m)
            vel[part, 2, j] = jnp.where(inside(part, j - 1, 2), vy_m + (2.0 * VELOCITY_STEP) * res / ay_m, 0.0)
            pz = tz - z_roll(tz, 1) + 0.25 * (y_roll(fzy, -1) - fzy)
            py = ty - y_roll(ty, 1) + 0.25 * (z_roll(fyz, -1) - fyz)
            return eta, tx, vz, vy, fzx, fyx, pz, py, az, ay, rho[part, j]

        loop(first_plane, last_plane + 1, stage, (zero,) * 11, (last_plane + 1 - first_plane) // 3)

    def odd(part):
        iteration(part, 0, PLANES - 2)

    def even(part):
        iteration(part, 1, PLANES - HIGH)

    def field(part, a, i):
        return vel[part, a, i + LOW + 1, 0:BZ] if a < 3 else pres[part, i + LOW, 0:BZ]

    for cp in main_copies:
        cp.wait_recv()
    unpack(unpack_first, 0, lambda a, j: first[a, j])
    odd(0)
    even(0)

    def repack_main(i, carry):
        for a in range(4):
            second[a, i + LOW, 0:BZ] = field(0, a, i)
        return carry

    loop(0, BX, repack_main, 0, 8)
    main_second = exchange(second, 0, 4, send_c, recv_c)

    for cp in halo_copies:
        cp.wait_recv()
    unpack(unpack_first, 1, strip_first)
    odd(1)
    even(1)

    def repack_strip(i, carry):
        packed = field(1, 0, i)
        place = lane_v + jnp.where(lane_v >= LEFT_AT, -LEFT_AT, BY - LEFT_AT)
        for a in range(1, 4):
            rolled = pltpu.roll(field(1, a, i), LEFT * a, 1)
            packed = jnp.where((place >= LEFT * a) & (place < LEFT * (a + 1)), rolled, packed)
        second[4, i + LOW, 0:BZ] = packed
        return carry

    loop(0, BX, repack_strip, 0, 8)
    strip_second_copies = exchange(second, 4, 1, send_d, recv_d)
    for a, b in SIDES:
        pl.semaphore_signal(here.at[0], inc=1, device_id=neighbour(2 * a, 2 * b, 0), device_id_type=MESH)

    for cp in main_second:
        cp.wait_recv()
    unpack(unpack_second, 0, lambda a, j: second[a, j])
    odd(0)
    for cp in strip_second_copies:
        cp.wait_recv()
    unpack(unpack_second, 1, strip_second)
    odd(1)

    def joined(main, strip):
        return jnp.where(lane_v < YLOW, pltpu.roll(strip, BY - SHIFT, 1), jnp.where(lane_v >= BY - YHIGH, strip, main))

    def last_pressure(i, total):
        j = i + LOW
        parts = []
        for part in range(2):
            vx = vel[part, 0, j + 1, 0:BZ]
            vz = vel[part, 1, j + 1]
            vy = vel[part, 2, j + 1, 0:BZ]
            rx = vel[part, 0, j + 2, 0:BZ] - vx
            rz = (z_roll(vz, -1) - vz)[0:BZ]
            ry = y_roll(vy, -1) - vy
            eta, div = viscosity(rx, rz, ry, pref[part, j, 0:BZ], expo[part, j, 0:BZ])
            parts.append((pres[part, j, 0:BZ] - PRESSURE_STEP * eta * div, eta))
        p, eta = (joined(main, strip) for main, strip in zip(*parts))
        last_p[i] = p
        last_eta[i] = eta
        return total + p

    total = loop(0, BX, last_pressure, jnp.zeros((BZ, BY), jnp.float32), 8)

    total = jnp.sum(total, axis=0, keepdims=True)
    eta_copy = pltpu.make_async_copy(last_eta, out_ref.at[4], out_sem.at[4])
    eta_copy.start()
    out_copies = [eta_copy]
    base = 0
    sum_sends = []
    for n, devices in enumerate(sum_phases):
        count = len(devices)
        ar_src[n] = total
        pl.semaphore_wait(here.at[n], len(SIDES))
        for o, d in enumerate(devices):
            pltpu.make_async_remote_copy(
                src_ref=ar_src.at[n], dst_ref=ar_buf.at[base + o], send_sem=ar_send.at[n], recv_sem=ar_recv.at[n],
                device_id=d, device_id_type=MESH).start()
        part = ar_buf.at[pl.ds(base, count)]
        sum_sends.append(pltpu.make_async_copy(part, part, ar_send.at[n]))
        if n == 0:
            for a, b in SIDES:
                pl.semaphore_signal(here.at[1], inc=1, device_id=neighbour(4 * a, 4 * b, 0), device_id_type=MESH)
            even(0)
            even(1)

            def join(i, carry):
                for a, comp in enumerate((0, 2, 1)):
                    last_v[a, i] = joined(field(0, comp, i), field(1, comp, i))
                return carry

            loop(0, BX, join, 0, 8)
            for a in range(3):
                cp = pltpu.make_async_copy(last_v.at[a], out_ref.at[a], out_sem.at[a])
                cp.start()
                out_copies.append(cp)
        pltpu.make_async_copy(part, part, ar_recv.at[n]).wait()
        for o in range(count):
            total = total + ar_buf[base + o]
        base += count
    cells = float(ngx * ngy * ngz * BX * BZ * BY)
    mean = jnp.sum(total) / cells
    last_p[...] = last_p[...] - mean
    p_copy = pltpu.make_async_copy(last_p, out_ref.at[3], out_sem.at[3])
    p_copy.start()
    out_copies.append(p_copy)

    for cp in y_copies + main_copies + halo_copies + main_second + strip_second_copies:
        cp.wait_send()
    for cp in sum_sends + out_copies:
        cp.wait()


def split_kernel(in_ref, *refs):
    *outs, held, sem_in, sem_out = refs
    into = [pltpu.make_async_copy(in_ref.at[n], held.at[n], sem_in.at[n]) for n in range(5)]
    back = [pltpu.make_async_copy(held.at[n], out, sem_out.at[n]) for n, out in enumerate(outs)]
    for cp in into:
        cp.start()
    for cp, after in zip(into, back):
        cp.wait()
        after.start()
    for cp in back:
        cp.wait()


def local(sizes, vel_x, vel_y, vel_z, pressure, phase, visc_scale, power_n, density):
    ngx, ngy, ngz, z_lo = sizes
    partners = (z_lo * ngy * 2 - 1) + (ngx // z_lo * (ngz // 2) - 1)
    f32 = jnp.float32
    hbm = pl.BlockSpec(memory_space=pltpu.HBM)
    dma = pltpu.SemaphoreType.DMA
    planes = (2, PLANES, ROWS, BY)
    stacked = pl.pallas_call(
        functools.partial(kernel, sizes),
        out_shape=jax.ShapeDtypeStruct((5, BX, BZ, BY), f32),
        in_specs=[hbm] * 8,
        out_specs=hbm,
        scratch_shapes=[
            pltpu.SMEM((PHASES,), f32),
            pltpu.SMEM((PHASES,), f32),
            pltpu.SMEM((PHASES,), f32),
            pltpu.VMEM((BX, BZ, BY), jnp.int32),
            pltpu.VMEM((6, PLANES, ROWS, BY), f32),
            pltpu.VMEM((5, PLANES, ROWS, BY), f32),
            pltpu.VMEM((2, BX // 2, BZ, BY), f32),
            pltpu.VMEM((2, BX // 2, BZ, BY), f32),
            pltpu.VMEM((2, 3, PLANES + 2, ROWS, BY), f32),
            pltpu.VMEM(planes, f32),
            pltpu.VMEM(planes, f32),
            pltpu.VMEM(planes, f32),
            pltpu.VMEM(planes, f32),
            pltpu.VMEM((3, BX, BZ, BY), f32),
            pltpu.VMEM((BX, BZ, BY), f32),
            pltpu.VMEM((BX, BZ, BY), f32),
            pltpu.VMEM((2, 1, BY), f32),
            pltpu.VMEM((partners, 1, BY), f32),
            dma((8,)), dma((2,)), dma((2,)),
            dma((8,)), dma((8,)), dma((8,)), dma((8,)), dma((8,)), dma((8,)), dma((8,)), dma((8,)),
            dma((2,)), dma((2,)), dma((5,)), pltpu.SemaphoreType.REGULAR((2,)),
        ],
        name="stokes",
        compiler_params=pltpu.CompilerParams(
            collective_id=0, has_side_effects=True, vmem_limit_bytes=VMEM_BYTES),
    )(vel_x, vel_y, vel_z, pressure, phase, visc_scale, power_n, density)
    return pl.pallas_call(
        split_kernel,
        out_shape=[jax.ShapeDtypeStruct((BX, BZ, BY), f32)] * 5,
        in_specs=[hbm],
        out_specs=[hbm] * 5,
        scratch_shapes=[pltpu.VMEM((5, BX, BZ, BY), f32), dma((5,)), dma((5,))],
        name="split",
        compiler_params=pltpu.CompilerParams(vmem_limit_bytes=VMEM_BYTES),
    )(stacked)


def solution(mesh, z_lo=Z_LO):
    sizes = (mesh.shape["gx"], mesh.shape["gy"], mesh.shape["gz"], z_lo)
    block = P("gx", "gz", "gy")
    return jax.shard_map(
        functools.partial(local, sizes),
        mesh=mesh,
        in_specs=(block,) * 5 + (P(),) * 3,
        out_specs=(block,) * 5,
        check_vma=False,
    )
```

```python
import functools
import itertools

import jax
import jax.numpy as jnp
from jax import lax
from jax.experimental import pallas as pl
from jax.experimental.pallas import tpu as pltpu
from jax.sharding import PartitionSpec as P

ITERS = 4
PHASES = 4
STRAIN_FLOOR = 1.0
PRESSURE_STEP = 0.5
VELOCITY_STEP = 0.1

BX, BZ, BY = 16, 8, 128
LOW, HIGH = 2, 4
YLOW, YHIGH = 4, 8
PLANES = BX + LOW + HIGH
ROWS = 2 * BZ
GROUP = YLOW + YHIGH
SHIFT = YHIGH + YLOW
UNPACK = 11
LEFT_AT, LEFT = 118, 30
Z_LO = 4
VMEM_BYTES = 62 * 1024 * 1024
MESH = pl.DeviceIdType.MESH

SIDES = ((-1, -1), (1, -1), (-1, 1), (1, 1), (-1, 0), (1, 0), (0, -1), (0, 1))


def send_planes(a):
    return {0: (LOW, BX), 1: (LOW + BX - LOW, LOW), -1: (LOW, HIGH)}[a]


def land_planes(a):
    return {0: LOW, 1: 0, -1: LOW + BX}[a]


def send_rows(b):
    return {0: (0, BZ), 1: (BZ - LOW, LOW), -1: (0, HIGH)}[b]


def land_rows(b):
    return {0: 0, 1: ROWS - LOW, -1: BZ}[b]


def loop(lower, upper, body, carry, unroll):
    assert (upper - lower) % unroll == 0

    def several(n, c):
        stores = []
        for u in range(unroll):
            c = body(lower + n * unroll + u, c, stores)
        for ref, place, value in stores:
            ref[place] = value
        return c

    return lax.fori_loop(0, (upper - lower) // unroll, several, carry)


def y_roll(x, s):
    return pltpu.roll(x, s % BY, 1)


def z_roll(x, s):
    return pltpu.roll(x, s % ROWS, 0)


def viscosity(rx, rz, ry, prefactor, power):
    div = rx + ry + rz
    third = div * (1.0 / 3.0)
    dx, dy, dz = rx - third, ry - third, rz - third
    inv = 0.5 * (dx * dx + dy * dy + dz * dz) + STRAIN_FLOOR
    return prefactor * jnp.exp(power * jnp.log(inv)), div


def kernel(sizes, vx_ref, vy_ref, vz_ref, p_ref, ph_ref, vs_in, pn_in, dn_in, out_ref,
           vs_ref, pn_ref, dn_ref, ph_in, first, second, s_pack, r_pack, vel, pres, pref, expo, rho, last_v, last_p, last_eta, ar_src, ar_buf,
           in_sem, ysend, yrecv, send_a, recv_a, send_b, recv_b, send_c, recv_c, send_d, recv_d, ar_send, ar_recv, out_sem, here):
    ngx, ngy, ngz, z_lo = sizes
    gx, gy, gz = lax.axis_index("gx"), lax.axis_index("gy"), lax.axis_index("gz")

    n_x, n_y, n_z = ngx // z_lo, ngz // 2, z_lo * ngy

    def neighbour(a, b, c):
        return (lax.rem(gx + (a + ngx), ngx), lax.rem(gy + (c + ngy), ngy), lax.rem(gz + (b + ngz), ngz))

    chip_x, chip_y, core = gx // z_lo, gz // 2, lax.rem(gz, 2)
    chip_z = gy * z_lo + lax.rem(gx, z_lo)

    def far(x, y, z, c):
        z = lax.rem(chip_z + z, n_z)
        return (lax.rem(chip_x + x, n_x) * z_lo + lax.rem(z, z_lo), z // z_lo,
                lax.rem(chip_y + y, n_y) * 2 + lax.rem(core + c, 2))

    def hops(o):
        return sum(min(d, n - d) for d, n in zip(o, (n_x, n_y, n_z, 2)))

    def group(*counts):
        offsets = [o for o in itertools.product(*[range(n) for n in counts]) if any(o)]
        return [far(*o) for o in sorted(offsets, key=hops, reverse=True)]

    sum_phases = (group(1, 1, n_z, 2), group(n_x, n_y, 1, 1))

    barrier = pltpu.get_barrier_semaphore()
    greeted = [neighbour(0, 0, -1), neighbour(0, 0, 1)] + [neighbour(a, b, 0) for a, b in SIDES]
    for d in greeted:
        pl.semaphore_signal(barrier, inc=1, device_id=d, device_id_type=MESH)

    in_copies = []
    for n, (src, dst) in enumerate(
        ((vx_ref, first.at[0, pl.ds(LOW, BX), pl.ds(0, BZ)]),
         (vz_ref, first.at[1, pl.ds(LOW, BX), pl.ds(0, BZ)]),
         (vy_ref, first.at[2, pl.ds(LOW, BX), pl.ds(0, BZ)]),
         (p_ref, first.at[3, pl.ds(LOW, BX), pl.ds(0, BZ)]),
         (ph_ref, ph_in), (vs_in, vs_ref), (pn_in, pn_ref), (dn_in, dn_ref))):
        cp = pltpu.make_async_copy(src, dst, in_sem.at[n])
        cp.start()
        in_copies.append(cp)


    lane_v = lax.broadcasted_iota(jnp.int32, (BZ, BY), 1)
    rows = pl.ds(0, BZ)
    for cp in in_copies:
        cp.wait()
    first[4, LOW:LOW + BX, 0:BZ] = ph_in[...].astype(jnp.float32)

    def pack(k, carry, stores):
        lo = jnp.zeros((BZ, BY), jnp.float32)
        hi = jnp.zeros((BZ, BY), jnp.float32)
        for q in range(2):
            for a in range(5):
                base = GROUP * a + 64 * q
                block = first[a, LOW + 2 * k + q, 0:BZ]
                rolled = pltpu.roll(block, base, 1) if base else block
                lo = jnp.where((lane_v >= base) & (lane_v < base + YHIGH), rolled, lo)
                rolled = pltpu.roll(block, base + SHIFT, 1)
                hi = jnp.where((lane_v >= base + YHIGH) & (lane_v < base + SHIFT), rolled, hi)
        stores += [(s_pack, (0, k), lo), (s_pack, (1, k), hi)]
        return carry

    loop(0, BX // 2, pack, 0, 4)
    pl.semaphore_wait(barrier, len(greeted))

    y_copies = []
    for n, c in enumerate((-1, 1)):
        cp = pltpu.make_async_remote_copy(
            src_ref=s_pack.at[n], dst_ref=r_pack.at[n], send_sem=ysend.at[n], recv_sem=yrecv.at[n],
            device_id=neighbour(0, 0, c), device_id_type=MESH)
        cp.start()
        y_copies.append(cp)

    def exchange(buf, lo, count, send, recv):
        copies = []
        for n, (a, b) in enumerate(SIDES):
            (p0, pn), (r0, rn) = send_planes(a), send_rows(b)
            cp = pltpu.make_async_remote_copy(
                src_ref=buf.at[pl.ds(lo, count), pl.ds(p0, pn), pl.ds(r0, rn)],
                dst_ref=buf.at[pl.ds(lo, count), pl.ds(land_planes(a), pn), pl.ds(land_rows(b), rn)],
                send_sem=send.at[n], recv_sem=recv.at[n],
                device_id=neighbour(a, b, 0), device_id_type=MESH)
            cp.start()
            copies.append(cp)
        return copies

    main_copies = exchange(first, 0, 5, send_a, recv_a)
    for cp in y_copies:
        cp.wait_recv()

    def unpack_y(k, carry, stores):
        both = jnp.where(lax.rem(lax.rem(lane_v, 64), GROUP) >= YHIGH, r_pack[1, k], r_pack[0, k])
        stores.append((first, (5, LOW + 2 * k, rows), both))
        stores.append((first, (5, LOW + 2 * k + 1, rows), pltpu.roll(both, 64, 1)))
        return carry

    loop(0, BX // 2, unpack_y, 0, 8)
    halo_copies = exchange(first, 5, 1, send_b, recv_b)

    full = (ROWS, BY)
    row = lax.broadcasted_iota(jnp.int32, full, 0)
    lane = lax.broadcasted_iota(jnp.int32, full, 1)
    zi = gz * BZ + jnp.where(row >= ROWS - LOW, row - ROWS, row)
    in_strip = jnp.where(lane < YHIGH, lane + BY, jnp.where(lane < BY // 2, lane - SHIFT, lane))
    in_z = (zi >= 0) & (zi < ngz * BZ)
    masks = []
    for cell in (lane, in_strip):
        yi = gy * BY + cell
        in_zy = in_z & (yi >= 0) & (yi < ngy * BY)
        masks.append({None: in_zy, 0: in_zy, 1: in_zy & (zi >= 1), 2: in_zy & (yi >= 1)})

    blank = jnp.zeros(full, jnp.float32)

    def x_ends(part, viscous):
        @pl.when(gx == 0)
        def _():
            for j in range(LOW):
                for a in range(3):
                    vel[part, a, j + 1] = blank
                if viscous:
                    pref[part, j] = blank
            vel[part, 0, LOW + 1] = blank

        @pl.when(gx == ngx - 1)
        def _():
            for j in range(LOW + BX, PLANES):
                for a in range(3):
                    vel[part, a, j + 1] = blank
                if viscous:
                    pref[part, j] = blank

    def splat(ref):
        return [jnp.full(full, ref[k], jnp.float32) for k in range(PHASES)]

    scales, powers, densities = splat(vs_ref), splat(pn_ref), splat(dn_ref)
    powers = [0.5 * (1.0 / n - 1.0) for n in powers]

    def select(phase, table):
        out = table[PHASES - 1]
        for k in range(PHASES - 2, -1, -1):
            out = jnp.where(phase == float(k), table[k], out)
        return out

    def unpack_second(part, j, whole, stores):
        for a in range(3):
            stores.append((vel, (part, a, j + 1), jnp.where(masks[part][a], whole(a, j), 0.0)))
        stores.append((pres, (part, j), whole(3, j)))

    def lookups(part, j, phase, stores):
        stores.append((pref, (part, j), jnp.where(masks[part][None], select(phase, scales), 0.0)))
        stores.append((expo, (part, j), select(phase, powers)))
        stores.append((rho, (part, j), select(phase, densities)))

    def main_first(j, carry, stores):
        unpack_second(0, j, lambda a, j: first[a, j], stores)
        lookups(0, j, first[4, j], stores)
        return carry

    def main_again(j, carry, stores):
        unpack_second(0, j, lambda a, j: second[a, j], stores)
        return carry

    def strip_own(j, carry, stores):
        for a in range(5):
            main = first[a, j]
            own = jnp.where(lane < BY // 2, pltpu.roll(main, SHIFT, 1), main)
            if a < 3:
                stores.append((vel, (1, a, j + 1), own))
            else:
                stores.append((pres if a == 3 else expo, (1, j), own))
        return carry

    def strip_halo(a):
        def body(j, carry, stores):
            halo = first[5, j]
            if a:
                halo = pltpu.roll(halo, BY - GROUP * a, 1)
            halo = jnp.where(lane < SHIFT, halo, vel[1, a, j + 1] if a < 3 else pres[1, j] if a == 3 else expo[1, j])
            if a < 3:
                stores.append((vel, (1, a, j + 1), jnp.where(masks[1][a], halo, 0.0)))
            elif a == 3:
                stores.append((pres, (1, j), halo))
            else:
                lookups(1, j, halo, stores)
            return carry

        return body

    def strip_again(j, carry, stores):
        def left(a, j):
            packed = second[4, j]
            return pltpu.roll(packed, BY - LEFT * a, 1) if a else packed

        unpack_second(1, j, left, stores)
        return carry

    def planes(body):
        loop(0, PLANES, body, 0, UNPACK)

    def iteration(part, first_plane, last_plane):
        def stage(j, carry, stores):
            eta_m, tx_m, vz_m, vy_m, fzx_m, fyx_m, pz_m, py_m, az_m, ay_m, rho_m = carry
            vx, vz, vy = vel[part, 0, j + 1], vel[part, 1, j + 1], vel[part, 2, j + 1]
            rx = vel[part, 0, j + 2] - vx
            rz = z_roll(vz, -1) - vz
            ry = y_roll(vy, -1) - vy
            eta, div = viscosity(rx, rz, ry, pref[part, j], expo[part, j])
            p = pres[part, j] - PRESSURE_STEP * eta * div
            stores.append((pres, (part, j), p))
            tx, tz, ty = eta * rx - p, eta * rz - p, eta * ry - p
            ax = eta + eta_m
            az = eta + z_roll(eta, 1)
            ay = eta + y_roll(eta, 1)
            exz = az + az_m
            exy = ay + ay_m
            eyz = ay + z_roll(ay, 1)
            fzx = exz * (vz - vz_m)
            fyx = exy * (vy - vy_m)
            fxz = exz * (vx - z_roll(vx, 1))
            fxy = exy * (vx - y_roll(vx, 1))
            fyz = eyz * (vy - z_roll(vy, 1))
            fzy = eyz * (vz - y_roll(vz, 1))
            res = tx - tx_m + 0.25 * ((z_roll(fxz, -1) - fxz) + (y_roll(fxy, -1) - fxy))
            new = jnp.where(masks[part][0], vx + (2.0 * VELOCITY_STEP) * res / ax, 0.0)
            stores.append((vel, (part, 0, j + 1), new))
            res = pz_m + 0.25 * (fzx - fzx_m) - rho_m
            new = jnp.where(masks[part][1], vz_m + (2.0 * VELOCITY_STEP) * res / az_m, 0.0)
            stores.append((vel, (part, 1, j), new))
            res = py_m + 0.25 * (fyx - fyx_m)
            new = jnp.where(masks[part][2], vy_m + (2.0 * VELOCITY_STEP) * res / ay_m, 0.0)
            stores.append((vel, (part, 2, j), new))
            pz = tz - z_roll(tz, 1) + 0.25 * (y_roll(fzy, -1) - fzy)
            py = ty - y_roll(ty, 1) + 0.25 * (z_roll(fyz, -1) - fyz)
            return eta, tx, vz, vy, fzx, fyx, pz, py, az, ay, rho[part, j]

        loop(first_plane, last_plane + 1, stage, (blank,) * 11, (last_plane + 1 - first_plane) // 3)
        x_ends(part, False)

    def odd(part):
        iteration(part, 0, PLANES - 2)

    def even(part):
        iteration(part, 1, PLANES - HIGH)

    def field(part, a, i):
        return vel[part, a, i + LOW + 1, 0:BZ] if a < 3 else pres[part, i + LOW, 0:BZ]

    for cp in main_copies:
        cp.wait_recv()
    planes(main_first)
    x_ends(0, True)
    odd(0)
    even(0)

    def repack_main(i, carry, stores):
        for a in range(4):
            stores.append((second, (a, i + LOW, rows), field(0, a, i)))
        return carry

    loop(0, BX, repack_main, 0, 8)
    main_second = exchange(second, 0, 4, send_c, recv_c)
    planes(strip_own)

    for cp in halo_copies:
        cp.wait_recv()
    for a in range(5):
        planes(strip_halo(a))
    x_ends(1, True)
    odd(1)
    even(1)

    def repack_strip(i, carry, stores):
        packed = field(1, 0, i)
        place = lane_v + jnp.where(lane_v >= LEFT_AT, -LEFT_AT, BY - LEFT_AT)
        for a in range(1, 4):
            rolled = pltpu.roll(field(1, a, i), LEFT * a, 1)
            packed = jnp.where((place >= LEFT * a) & (place < LEFT * (a + 1)), rolled, packed)
        stores.append((second, (4, i + LOW, rows), packed))
        return carry

    loop(0, BX, repack_strip, 0, 8)
    strip_second_copies = exchange(second, 4, 1, send_d, recv_d)
    for a, b in SIDES:
        pl.semaphore_signal(here.at[0], inc=1, device_id=neighbour(2 * a, 2 * b, 0), device_id_type=MESH)

    for cp in main_second:
        cp.wait_recv()
    planes(main_again)
    x_ends(0, False)
    odd(0)
    for cp in strip_second_copies:
        cp.wait_recv()
    planes(strip_again)
    x_ends(1, False)
    odd(1)

    def joined(main, strip):
        return jnp.where(lane_v < YLOW, pltpu.roll(strip, BY - SHIFT, 1), jnp.where(lane_v >= BY - YHIGH, strip, main))

    def last_pressure(i, total, stores):
        j = i + LOW
        parts = []
        for part in range(2):
            vx = vel[part, 0, j + 1, 0:BZ]
            vz = vel[part, 1, j + 1]
            vy = vel[part, 2, j + 1, 0:BZ]
            rx = vel[part, 0, j + 2, 0:BZ] - vx
            rz = (z_roll(vz, -1) - vz)[0:BZ]
            ry = y_roll(vy, -1) - vy
            eta, div = viscosity(rx, rz, ry, pref[part, j, 0:BZ], expo[part, j, 0:BZ])
            parts.append((pres[part, j, 0:BZ] - PRESSURE_STEP * eta * div, eta))
        p, eta = (joined(main, strip) for main, strip in zip(*parts))
        stores += [(last_p, i, p), (last_eta, i, eta)]
        return total + p

    total = loop(0, BX, last_pressure, jnp.zeros((BZ, BY), jnp.float32), 8)

    total = jnp.sum(total, axis=0, keepdims=True)
    eta_copy = pltpu.make_async_copy(last_eta, out_ref.at[4], out_sem.at[4])
    eta_copy.start()
    out_copies = [eta_copy]
    base = 0
    sum_sends = []
    for n, devices in enumerate(sum_phases):
        count = len(devices)
        ar_src[n] = total
        pl.semaphore_wait(here.at[n], len(SIDES))
        for o, d in enumerate(devices):
            pltpu.make_async_remote_copy(
                src_ref=ar_src.at[n], dst_ref=ar_buf.at[base + o], send_sem=ar_send.at[n], recv_sem=ar_recv.at[n],
                device_id=d, device_id_type=MESH).start()
        part = ar_buf.at[pl.ds(base, count)]
        sum_sends.append(pltpu.make_async_copy(part, part, ar_send.at[n]))
        if n == 0:
            for a, b in SIDES:
                pl.semaphore_signal(here.at[1], inc=1, device_id=neighbour(4 * a, 4 * b, 0), device_id_type=MESH)
            even(0)
            even(1)

            def join(i, carry, stores):
                for a, comp in enumerate((0, 2, 1)):
                    stores.append((last_v, (a, i), joined(field(0, comp, i), field(1, comp, i))))
                return carry

            loop(0, BX, join, 0, 8)
            for a in range(3):
                cp = pltpu.make_async_copy(last_v.at[a], out_ref.at[a], out_sem.at[a])
                cp.start()
                out_copies.append(cp)
        pltpu.make_async_copy(part, part, ar_recv.at[n]).wait()
        for o in range(count):
            total = total + ar_buf[base + o]
        base += count
    cells = float(ngx * ngy * ngz * BX * BZ * BY)
    mean = jnp.sum(total) / cells
    last_p[...] = last_p[...] - mean
    p_copy = pltpu.make_async_copy(last_p, out_ref.at[3], out_sem.at[3])
    p_copy.start()
    out_copies.append(p_copy)

    for cp in y_copies + main_copies + halo_copies + main_second + strip_second_copies:
        cp.wait_send()
    for cp in sum_sends + out_copies:
        cp.wait()


def split_kernel(in_ref, *refs):
    *outs, held, sem_in, sem_out = refs
    into = [pltpu.make_async_copy(in_ref.at[n], held.at[n], sem_in.at[n]) for n in range(5)]
    back = [pltpu.make_async_copy(held.at[n], out, sem_out.at[n]) for n, out in enumerate(outs)]
    for cp in into:
        cp.start()
    for cp, after in zip(into, back):
        cp.wait()
        after.start()
    for cp in back:
        cp.wait()


def local(sizes, vel_x, vel_y, vel_z, pressure, phase, visc_scale, power_n, density):
    ngx, ngy, ngz, z_lo = sizes
    partners = (z_lo * ngy * 2 - 1) + (ngx // z_lo * (ngz // 2) - 1)
    f32 = jnp.float32
    hbm = pl.BlockSpec(memory_space=pltpu.HBM)
    dma = pltpu.SemaphoreType.DMA
    planes = (2, PLANES, ROWS, BY)
    stacked = pl.pallas_call(
        functools.partial(kernel, sizes),
        out_shape=jax.ShapeDtypeStruct((5, BX, BZ, BY), f32),
        in_specs=[hbm] * 8,
        out_specs=hbm,
        scratch_shapes=[
            pltpu.SMEM((PHASES,), f32),
            pltpu.SMEM((PHASES,), f32),
            pltpu.SMEM((PHASES,), f32),
            pltpu.VMEM((BX, BZ, BY), jnp.int32),
            pltpu.VMEM((6, PLANES, ROWS, BY), f32),
            pltpu.VMEM((5, PLANES, ROWS, BY), f32),
            pltpu.VMEM((2, BX // 2, BZ, BY), f32),
            pltpu.VMEM((2, BX // 2, BZ, BY), f32),
            pltpu.VMEM((2, 3, PLANES + 2, ROWS, BY), f32),
            pltpu.VMEM(planes, f32),
            pltpu.VMEM(planes, f32),
            pltpu.VMEM(planes, f32),
            pltpu.VMEM(planes, f32),
            pltpu.VMEM((3, BX, BZ, BY), f32),
            pltpu.VMEM((BX, BZ, BY), f32),
            pltpu.VMEM((BX, BZ, BY), f32),
            pltpu.VMEM((2, 1, BY), f32),
            pltpu.VMEM((partners, 1, BY), f32),
            dma((8,)), dma((2,)), dma((2,)),
            dma((8,)), dma((8,)), dma((8,)), dma((8,)), dma((8,)), dma((8,)), dma((8,)), dma((8,)),
            dma((2,)), dma((2,)), dma((5,)), pltpu.SemaphoreType.REGULAR((2,)),
        ],
        name="stokes",
        compiler_params=pltpu.CompilerParams(
            collective_id=0, has_side_effects=True, vmem_limit_bytes=VMEM_BYTES),
    )(vel_x, vel_y, vel_z, pressure, phase, visc_scale, power_n, density)
    return pl.pallas_call(
        split_kernel,
        out_shape=[jax.ShapeDtypeStruct((BX, BZ, BY), f32)] * 5,
        in_specs=[hbm],
        out_specs=[hbm] * 5,
        scratch_shapes=[pltpu.VMEM((5, BX, BZ, BY), f32), dma((5,)), dma((5,))],
        name="split",
        compiler_params=pltpu.CompilerParams(vmem_limit_bytes=VMEM_BYTES),
    )(stacked)


def solution(mesh, z_lo=Z_LO):
    sizes = (mesh.shape["gx"], mesh.shape["gy"], mesh.shape["gz"], z_lo)
    block = P("gx", "gz", "gy")
    return jax.shard_map(
        functools.partial(local, sizes),
        mesh=mesh,
        in_specs=(block,) * 5 + (P(),) * 3,
        out_specs=(block,) * 5,
        check_vma=False,
    )
```

```python
import functools
import itertools

import jax
import jax.numpy as jnp
from jax import lax
from jax.experimental import pallas as pl
from jax.experimental.pallas import tpu as pltpu
from jax.sharding import PartitionSpec as P

ITERS = 4
PHASES = 4
STRAIN_FLOOR = 1.0
PRESSURE_STEP = 0.5
VELOCITY_STEP = 0.1

BX, BZ, BY = 16, 8, 128
LOW, HIGH = 2, 4
YLOW, YHIGH = 4, 8
PLANES = BX + LOW + HIGH
ROWS = 2 * BZ
GROUP = YLOW + YHIGH
SHIFT = YHIGH + YLOW
UNPACK = 11
LEFT_AT, LEFT = 118, 30
Z_LO = 4
VMEM_BYTES = 62 * 1024 * 1024
MESH = pl.DeviceIdType.MESH

SIDES = ((-1, -1), (1, -1), (-1, 1), (1, 1), (-1, 0), (1, 0), (0, -1), (0, 1))


def send_planes(a):
    return {0: (LOW, BX), 1: (LOW + BX - LOW, LOW), -1: (LOW, HIGH)}[a]


def land_planes(a):
    return {0: LOW, 1: 0, -1: LOW + BX}[a]


def send_rows(b):
    return {0: (0, BZ), 1: (BZ - LOW, LOW), -1: (0, HIGH)}[b]


def land_rows(b):
    return {0: 0, 1: ROWS - LOW, -1: BZ}[b]


def loop(lower, upper, body, carry, unroll):
    assert (upper - lower) % unroll == 0

    def several(n, c):
        stores = []
        for u in range(unroll):
            c = body(lower + n * unroll + u, c, stores)
        for ref, place, value in stores:
            ref[place] = value
        return c

    return lax.fori_loop(0, (upper - lower) // unroll, several, carry)


def y_roll(x, s):
    return pltpu.roll(x, s % BY, 1)


def z_roll(x, s):
    return pltpu.roll(x, s % ROWS, 0)


def viscosity(rx, rz, ry, prefactor, power):
    div = rx + ry + rz
    third = div * (1.0 / 3.0)
    dx, dy, dz = rx - third, ry - third, rz - third
    inv = 0.5 * (dx * dx + dy * dy + dz * dz) + STRAIN_FLOOR
    return prefactor * jnp.exp(power * jnp.log(inv)), div


def kernel(sizes, vx_ref, vy_ref, vz_ref, p_ref, ph_ref, vs_in, pn_in, dn_in, out_ref,
           vs_ref, pn_ref, dn_ref, ph_in, first, second, s_pack, r_pack, vel, pres, pref, expo, rho, ar_src, ar_buf,
           in_sem, ysend, yrecv, send_a, recv_a, send_b, recv_b, send_c, recv_c, send_d, recv_d, ar_send, ar_recv, here):
    ngx, ngy, ngz, z_lo = sizes
    gx, gy, gz = lax.axis_index("gx"), lax.axis_index("gy"), lax.axis_index("gz")

    n_x, n_y, n_z = ngx // z_lo, ngz // 2, z_lo * ngy

    def neighbour(a, b, c):
        return (lax.rem(gx + (a + ngx), ngx), lax.rem(gy + (c + ngy), ngy), lax.rem(gz + (b + ngz), ngz))

    chip_x, chip_y, core = gx // z_lo, gz // 2, lax.rem(gz, 2)
    chip_z = gy * z_lo + lax.rem(gx, z_lo)

    def far(x, y, z, c):
        z = lax.rem(chip_z + z, n_z)
        return (lax.rem(chip_x + x, n_x) * z_lo + lax.rem(z, z_lo), z // z_lo,
                lax.rem(chip_y + y, n_y) * 2 + lax.rem(core + c, 2))

    def hops(o):
        return sum(min(d, n - d) for d, n in zip(o, (n_x, n_y, n_z, 2)))

    def group(*counts):
        offsets = [o for o in itertools.product(*[range(n) for n in counts]) if any(o)]
        return [far(*o) for o in sorted(offsets, key=hops, reverse=True)]

    sum_phases = (group(1, 1, n_z, 2), group(n_x, n_y, 1, 1))

    barrier = pltpu.get_barrier_semaphore()
    greeted = [neighbour(0, 0, -1), neighbour(0, 0, 1)] + [neighbour(a, b, 0) for a, b in SIDES]
    for d in greeted:
        pl.semaphore_signal(barrier, inc=1, device_id=d, device_id_type=MESH)

    in_copies = []
    for n, (src, dst) in enumerate(
        ((vx_ref, first.at[0, pl.ds(LOW, BX), pl.ds(0, BZ)]),
         (vz_ref, first.at[1, pl.ds(LOW, BX), pl.ds(0, BZ)]),
         (vy_ref, first.at[2, pl.ds(LOW, BX), pl.ds(0, BZ)]),
         (p_ref, first.at[3, pl.ds(LOW, BX), pl.ds(0, BZ)]),
         (ph_ref, ph_in), (vs_in, vs_ref), (pn_in, pn_ref), (dn_in, dn_ref))):
        cp = pltpu.make_async_copy(src, dst, in_sem.at[n])
        cp.start()
        in_copies.append(cp)


    lane_v = lax.broadcasted_iota(jnp.int32, (BZ, BY), 1)
    rows = pl.ds(0, BZ)
    for cp in in_copies:
        cp.wait()
    first[4, LOW:LOW + BX, 0:BZ] = ph_in[...].astype(jnp.float32)

    def pack(k, carry, stores):
        lo = jnp.zeros((BZ, BY), jnp.float32)
        hi = jnp.zeros((BZ, BY), jnp.float32)
        for q in range(2):
            for a in range(5):
                base = GROUP * a + 64 * q
                block = first[a, LOW + 2 * k + q, 0:BZ]
                rolled = pltpu.roll(block, base, 1) if base else block
                lo = jnp.where((lane_v >= base) & (lane_v < base + YHIGH), rolled, lo)
                rolled = pltpu.roll(block, base + SHIFT, 1)
                hi = jnp.where((lane_v >= base + YHIGH) & (lane_v < base + SHIFT), rolled, hi)
        stores += [(s_pack, (0, k), lo), (s_pack, (1, k), hi)]
        return carry

    loop(0, BX // 2, pack, 0, 4)
    pl.semaphore_wait(barrier, len(greeted))

    y_copies = []
    for n, c in enumerate((-1, 1)):
        cp = pltpu.make_async_remote_copy(
            src_ref=s_pack.at[n], dst_ref=r_pack.at[n], send_sem=ysend.at[n], recv_sem=yrecv.at[n],
            device_id=neighbour(0, 0, c), device_id_type=MESH)
        cp.start()
        y_copies.append(cp)

    def exchange(buf, lo, count, send, recv):
        copies = []
        for n, (a, b) in enumerate(SIDES):
            (p0, pn), (r0, rn) = send_planes(a), send_rows(b)
            cp = pltpu.make_async_remote_copy(
                src_ref=buf.at[pl.ds(lo, count), pl.ds(p0, pn), pl.ds(r0, rn)],
                dst_ref=buf.at[pl.ds(lo, count), pl.ds(land_planes(a), pn), pl.ds(land_rows(b), rn)],
                send_sem=send.at[n], recv_sem=recv.at[n],
                device_id=neighbour(a, b, 0), device_id_type=MESH)
            cp.start()
            copies.append(cp)
        return copies

    main_copies = exchange(first, 0, 5, send_a, recv_a)
    for cp in y_copies:
        cp.wait_recv()

    def unpack_y(k, carry, stores):
        both = jnp.where(lax.rem(lax.rem(lane_v, 64), GROUP) >= YHIGH, r_pack[1, k], r_pack[0, k])
        stores.append((first, (5, LOW + 2 * k, rows), both))
        stores.append((first, (5, LOW + 2 * k + 1, rows), pltpu.roll(both, 64, 1)))
        return carry

    loop(0, BX // 2, unpack_y, 0, 8)
    halo_copies = exchange(first, 5, 1, send_b, recv_b)

    full = (ROWS, BY)
    row = lax.broadcasted_iota(jnp.int32, full, 0)
    lane = lax.broadcasted_iota(jnp.int32, full, 1)
    zi = gz * BZ + jnp.where(row >= ROWS - LOW, row - ROWS, row)
    in_strip = jnp.where(lane < YHIGH, lane + BY, jnp.where(lane < BY // 2, lane - SHIFT, lane))
    in_z = (zi >= 0) & (zi < ngz * BZ)
    masks = []
    for cell in (lane, in_strip):
        yi = gy * BY + cell
        in_zy = in_z & (yi >= 0) & (yi < ngy * BY)
        masks.append({None: in_zy, 0: in_zy, 1: in_zy & (zi >= 1), 2: in_zy & (yi >= 1)})

    blank = jnp.zeros(full, jnp.float32)

    def x_ends(part, viscous):
        @pl.when(gx == 0)
        def _():
            for j in range(LOW):
                for a in range(3):
                    vel[part, a, j + 1] = blank
                if viscous:
                    pref[part, j] = blank
            vel[part, 0, LOW + 1] = blank

        @pl.when(gx == ngx - 1)
        def _():
            for j in range(LOW + BX, PLANES):
                for a in range(3):
                    vel[part, a, j + 1] = blank
                if viscous:
                    pref[part, j] = blank

    def splat(ref):
        return [jnp.full(full, ref[k], jnp.float32) for k in range(PHASES)]

    scales, powers, densities = splat(vs_ref), splat(pn_ref), splat(dn_ref)
    powers = [0.5 * (1.0 / n - 1.0) for n in powers]

    def select(phase, table):
        out = table[PHASES - 1]
        for k in range(PHASES - 2, -1, -1):
            out = jnp.where(phase == float(k), table[k], out)
        return out

    def unpack_second(part, j, whole, stores):
        for a in range(3):
            stores.append((vel, (part, a, j + 1), jnp.where(masks[part][a], whole(a, j), 0.0)))
        stores.append((pres, (part, j), whole(3, j)))

    def lookups(part, j, phase, stores):
        stores.append((pref, (part, j), jnp.where(masks[part][None], select(phase, scales), 0.0)))
        stores.append((expo, (part, j), select(phase, powers)))
        stores.append((rho, (part, j), select(phase, densities)))

    def main_first(j, carry, stores):
        unpack_second(0, j, lambda a, j: first[a, j], stores)
        lookups(0, j, first[4, j], stores)
        return carry

    def main_again(j, carry, stores):
        unpack_second(0, j, lambda a, j: second[a, j], stores)
        return carry

    def strip_own(j, carry, stores):
        for a in range(5):
            main = first[a, j]
            own = jnp.where(lane < BY // 2, pltpu.roll(main, SHIFT, 1), main)
            if a < 3:
                stores.append((vel, (1, a, j + 1), own))
            else:
                stores.append((pres if a == 3 else expo, (1, j), own))
        return carry

    def strip_halo(a):
        def body(j, carry, stores):
            halo = first[5, j]
            if a:
                halo = pltpu.roll(halo, BY - GROUP * a, 1)
            halo = jnp.where(lane < SHIFT, halo, vel[1, a, j + 1] if a < 3 else pres[1, j] if a == 3 else expo[1, j])
            if a < 3:
                stores.append((vel, (1, a, j + 1), jnp.where(masks[1][a], halo, 0.0)))
            elif a == 3:
                stores.append((pres, (1, j), halo))
            else:
                lookups(1, j, halo, stores)
            return carry

        return body

    def strip_again(j, carry, stores):
        def left(a, j):
            packed = second[4, j]
            return pltpu.roll(packed, BY - LEFT * a, 1) if a else packed

        unpack_second(1, j, left, stores)
        return carry

    def planes(body):
        loop(0, PLANES, body, 0, UNPACK)

    def iteration(part, first_plane, last_plane):
        def stage(j, carry, stores):
            eta_m, tx_m, vz_m, vy_m, fzx_m, fyx_m, pz_m, py_m, az_m, ay_m, rho_m = carry
            vx, vz, vy = vel[part, 0, j + 1], vel[part, 1, j + 1], vel[part, 2, j + 1]
            rx = vel[part, 0, j + 2] - vx
            rz = z_roll(vz, -1) - vz
            ry = y_roll(vy, -1) - vy
            eta, div = viscosity(rx, rz, ry, pref[part, j], expo[part, j])
            p = pres[part, j] - PRESSURE_STEP * eta * div
            stores.append((pres, (part, j), p))
            tx, tz, ty = eta * rx - p, eta * rz - p, eta * ry - p
            ax = eta + eta_m
            az = eta + z_roll(eta, 1)
            ay = eta + y_roll(eta, 1)
            exz = az + az_m
            exy = ay + ay_m
            eyz = ay + z_roll(ay, 1)
            fzx = exz * (vz - vz_m)
            fyx = exy * (vy - vy_m)
            fxz = exz * (vx - z_roll(vx, 1))
            fxy = exy * (vx - y_roll(vx, 1))
            fyz = eyz * (vy - z_roll(vy, 1))
            fzy = eyz * (vz - y_roll(vz, 1))
            res = tx - tx_m + 0.25 * ((z_roll(fxz, -1) - fxz) + (y_roll(fxy, -1) - fxy))
            new = jnp.where(masks[part][0], vx + (2.0 * VELOCITY_STEP) * res / ax, 0.0)
            stores.append((vel, (part, 0, j + 1), new))
            res = pz_m + 0.25 * (fzx - fzx_m) - rho_m
            new = jnp.where(masks[part][1], vz_m + (2.0 * VELOCITY_STEP) * res / az_m, 0.0)
            stores.append((vel, (part, 1, j), new))
            res = py_m + 0.25 * (fyx - fyx_m)
            new = jnp.where(masks[part][2], vy_m + (2.0 * VELOCITY_STEP) * res / ay_m, 0.0)
            stores.append((vel, (part, 2, j), new))
            pz = tz - z_roll(tz, 1) + 0.25 * (y_roll(fzy, -1) - fzy)
            py = ty - y_roll(ty, 1) + 0.25 * (z_roll(fyz, -1) - fyz)
            return eta, tx, vz, vy, fzx, fyx, pz, py, az, ay, rho[part, j]

        loop(first_plane, last_plane + 1, stage, (blank,) * 11, last_plane + 1 - first_plane)
        x_ends(part, False)

    def odd(part):
        iteration(part, 0, PLANES - 2)

    def even(part):
        iteration(part, 1, PLANES - HIGH)

    def field(part, a, i):
        return vel[part, a, i + LOW + 1, 0:BZ] if a < 3 else pres[part, i + LOW, 0:BZ]

    for cp in main_copies:
        cp.wait_recv()
    planes(main_first)
    x_ends(0, True)
    odd(0)
    even(0)

    def repack_main(i, carry, stores):
        for a in range(4):
            stores.append((second, (a, i + LOW, rows), field(0, a, i)))
        return carry

    loop(0, BX, repack_main, 0, 8)
    main_second = exchange(second, 0, 4, send_c, recv_c)
    planes(strip_own)

    for cp in halo_copies:
        cp.wait_recv()
    for a in range(5):
        planes(strip_halo(a))
    x_ends(1, True)
    odd(1)
    even(1)

    def repack_strip(i, carry, stores):
        packed = field(1, 0, i)
        place = lane_v + jnp.where(lane_v >= LEFT_AT, -LEFT_AT, BY - LEFT_AT)
        for a in range(1, 4):
            rolled = pltpu.roll(field(1, a, i), LEFT * a, 1)
            packed = jnp.where((place >= LEFT * a) & (place < LEFT * (a + 1)), rolled, packed)
        stores.append((second, (4, i + LOW, rows), packed))
        return carry

    loop(0, BX, repack_strip, 0, 8)
    strip_second_copies = exchange(second, 4, 1, send_d, recv_d)
    for a, b in SIDES:
        pl.semaphore_signal(here.at[0], inc=1, device_id=neighbour(2 * a, 2 * b, 0), device_id_type=MESH)

    for cp in main_second:
        cp.wait_recv()
    planes(main_again)
    x_ends(0, False)
    odd(0)
    for cp in strip_second_copies:
        cp.wait_recv()
    planes(strip_again)
    x_ends(1, False)
    odd(1)

    def joined(main, strip):
        return jnp.where(lane_v < YLOW, pltpu.roll(strip, BY - SHIFT, 1), jnp.where(lane_v >= BY - YHIGH, strip, main))

    def last_pressure(i, total, stores):
        j = i + LOW
        parts = []
        for part in range(2):
            vx = vel[part, 0, j + 1, 0:BZ]
            vz = vel[part, 1, j + 1]
            vy = vel[part, 2, j + 1, 0:BZ]
            rx = vel[part, 0, j + 2, 0:BZ] - vx
            rz = (z_roll(vz, -1) - vz)[0:BZ]
            ry = y_roll(vy, -1) - vy
            eta, div = viscosity(rx, rz, ry, pref[part, j, 0:BZ], expo[part, j, 0:BZ])
            parts.append((pres[part, j, 0:BZ] - PRESSURE_STEP * eta * div, eta))
        p, eta = (joined(main, strip) for main, strip in zip(*parts))
        stores += [(out_ref, (3, i), p), (out_ref, (4, i), eta)]
        return total + p

    total = loop(0, BX, last_pressure, jnp.zeros((BZ, BY), jnp.float32), 8)

    total = jnp.sum(total, axis=0, keepdims=True)
    base = 0
    sum_sends = []
    for n, devices in enumerate(sum_phases):
        count = len(devices)
        ar_src[n] = total
        pl.semaphore_wait(here.at[n], len(SIDES))
        for o, d in enumerate(devices):
            pltpu.make_async_remote_copy(
                src_ref=ar_src.at[n], dst_ref=ar_buf.at[base + o], send_sem=ar_send.at[n], recv_sem=ar_recv.at[n],
                device_id=d, device_id_type=MESH).start()
        part = ar_buf.at[pl.ds(base, count)]
        sum_sends.append(pltpu.make_async_copy(part, part, ar_send.at[n]))
        if n == 0:
            for a, b in SIDES:
                pl.semaphore_signal(here.at[1], inc=1, device_id=neighbour(4 * a, 4 * b, 0), device_id_type=MESH)
            even(0)
            even(1)

            def join(i, carry, stores):
                for a, comp in enumerate((0, 2, 1)):
                    stores.append((out_ref, (a, i), joined(field(0, comp, i), field(1, comp, i))))
                return carry

            loop(0, BX, join, 0, 8)
        pltpu.make_async_copy(part, part, ar_recv.at[n]).wait()
        for o in range(count):
            total = total + ar_buf[base + o]
        base += count
    cells = float(ngx * ngy * ngz * BX * BZ * BY)
    mean = jnp.sum(total) / cells
    out_ref[3] = out_ref[3] - mean

    for cp in y_copies + main_copies + halo_copies + main_second + strip_second_copies:
        cp.wait_send()
    for cp in sum_sends:
        cp.wait()


def split_kernel(in_ref, *refs):
    *outs, sem = refs
    copies = [pltpu.make_async_copy(in_ref.at[n], out, sem.at[n]) for n, out in enumerate(outs)]
    for cp in copies:
        cp.start()
    for cp in copies:
        cp.wait()


def local(sizes, vel_x, vel_y, vel_z, pressure, phase, visc_scale, power_n, density):
    ngx, ngy, ngz, z_lo = sizes
    partners = (z_lo * ngy * 2 - 1) + (ngx // z_lo * (ngz // 2) - 1)
    f32 = jnp.float32
    hbm = pl.BlockSpec(memory_space=pltpu.HBM)
    dma = pltpu.SemaphoreType.DMA
    planes = (2, PLANES, ROWS, BY)
    stacked = pl.pallas_call(
        functools.partial(kernel, sizes),
        out_shape=pltpu.VMEM((5, BX, BZ, BY), f32),
        in_specs=[hbm] * 8,
        out_specs=pl.BlockSpec(memory_space=pltpu.VMEM),
        scratch_shapes=[
            pltpu.SMEM((PHASES,), f32),
            pltpu.SMEM((PHASES,), f32),
            pltpu.SMEM((PHASES,), f32),
            pltpu.VMEM((BX, BZ, BY), jnp.int32),
            pltpu.VMEM((6, PLANES, ROWS, BY), f32),
            pltpu.VMEM((5, PLANES, ROWS, BY), f32),
            pltpu.VMEM((2, BX // 2, BZ, BY), f32),
            pltpu.VMEM((2, BX // 2, BZ, BY), f32),
            pltpu.VMEM((2, 3, PLANES + 2, ROWS, BY), f32),
            pltpu.VMEM(planes, f32),
            pltpu.VMEM(planes, f32),
            pltpu.VMEM(planes, f32),
            pltpu.VMEM(planes, f32),
            pltpu.VMEM((2, 1, BY), f32),
            pltpu.VMEM((partners, 1, BY), f32),
            dma((8,)), dma((2,)), dma((2,)),
            dma((8,)), dma((8,)), dma((8,)), dma((8,)), dma((8,)), dma((8,)), dma((8,)), dma((8,)),
            dma((2,)), dma((2,)), pltpu.SemaphoreType.REGULAR((2,)),
        ],
        name="stokes",
        compiler_params=pltpu.CompilerParams(
            collective_id=0, has_side_effects=True, vmem_limit_bytes=VMEM_BYTES),
    )(vel_x, vel_y, vel_z, pressure, phase, visc_scale, power_n, density)
    return pl.pallas_call(
        split_kernel,
        out_shape=[jax.ShapeDtypeStruct((BX, BZ, BY), f32)] * 5,
        in_specs=[pl.BlockSpec(memory_space=pl.ANY)],
        out_specs=[hbm] * 5,
        scratch_shapes=[dma((5,))],
        name="split",
        compiler_params=pltpu.CompilerParams(vmem_limit_bytes=2 * 1024 * 1024),
    )(stacked)


def solution(mesh, z_lo=Z_LO):
    sizes = (mesh.shape["gx"], mesh.shape["gy"], mesh.shape["gz"], z_lo)
    block = P("gx", "gz", "gy")
    return jax.shard_map(
        functools.partial(local, sizes),
        mesh=mesh,
        in_specs=(block,) * 5 + (P(),) * 3,
        out_specs=(block,) * 5,
        check_vma=False,
    )
```

```python
import functools
import itertools

import jax
import jax.numpy as jnp
from jax import lax
from jax.experimental import pallas as pl
from jax.experimental.pallas import tpu as pltpu
from jax.sharding import PartitionSpec as P

ITERS = 4
PHASES = 4
STRAIN_FLOOR = 1.0
PRESSURE_STEP = 0.5
VELOCITY_STEP = 0.1

BX, BZ, BY = 16, 8, 128
LOW, HIGH = 2, 4
YLOW, YHIGH = 4, 8
PLANES = BX + LOW + HIGH
ROWS = 2 * BZ
GROUP = YLOW + YHIGH
SHIFT = YHIGH + YLOW
UNPACK = 22
LEFT_AT, LEFT = 118, 30
Z_LO = 4
VMEM_BYTES = 62 * 1024 * 1024
MESH = pl.DeviceIdType.MESH

SIDES = ((-1, -1), (1, -1), (-1, 1), (1, 1), (-1, 0), (1, 0), (0, -1), (0, 1))


def send_planes(a):
    return {0: (LOW, BX), 1: (LOW + BX - LOW, LOW), -1: (LOW, HIGH)}[a]


def land_planes(a):
    return {0: LOW, 1: 0, -1: LOW + BX}[a]


def send_rows(b):
    return {0: (0, BZ), 1: (BZ - LOW, LOW), -1: (0, HIGH)}[b]


def land_rows(b):
    return {0: 0, 1: ROWS - LOW, -1: BZ}[b]


def loop(lower, upper, body, carry, unroll):
    assert (upper - lower) % unroll == 0

    def several(n, c):
        stores = []
        for u in range(unroll):
            c = body(lower + n * unroll + u, c, stores)
        for ref, place, value in stores:
            ref[place] = value
        return c

    return lax.fori_loop(0, (upper - lower) // unroll, several, carry)


def y_roll(x, s):
    return pltpu.roll(x, s % BY, 1)


def z_roll(x, s):
    return pltpu.roll(x, s % ROWS, 0)


def viscosity(rx, rz, ry, prefactor, power):
    div = rx + ry + rz
    third = div * (1.0 / 3.0)
    dx, dy, dz = rx - third, ry - third, rz - third
    inv = 0.5 * (dx * dx + dy * dy + dz * dz) + STRAIN_FLOOR
    return prefactor * jnp.exp(power * jnp.log(inv)), div


def kernel(sizes, vx_ref, vy_ref, vz_ref, p_ref, ph_ref, vs_in, pn_in, dn_in, out_ref,
           vs_ref, pn_ref, dn_ref, ph_in, first, second, s_pack, r_pack, vel, pres, pref, expo, rho, last, ar_src, ar_buf,
           in_sem, ysend, yrecv, send_a, recv_a, send_b, recv_b, send_c, recv_c, send_d, recv_d, ar_send, ar_recv, here):
    ngx, ngy, ngz, z_lo = sizes
    gx, gy, gz = lax.axis_index("gx"), lax.axis_index("gy"), lax.axis_index("gz")

    n_x, n_y, n_z = ngx // z_lo, ngz // 2, z_lo * ngy

    def neighbour(a, b, c):
        return (lax.rem(gx + (a + ngx), ngx), lax.rem(gy + (c + ngy), ngy), lax.rem(gz + (b + ngz), ngz))

    chip_x, chip_y, core = gx // z_lo, gz // 2, lax.rem(gz, 2)
    chip_z = gy * z_lo + lax.rem(gx, z_lo)

    def far(x, y, z, c):
        z = lax.rem(chip_z + z, n_z)
        return (lax.rem(chip_x + x, n_x) * z_lo + lax.rem(z, z_lo), z // z_lo,
                lax.rem(chip_y + y, n_y) * 2 + lax.rem(core + c, 2))

    def hops(o):
        return sum(min(d, n - d) for d, n in zip(o, (n_x, n_y, n_z, 2)))

    def group(*counts):
        offsets = [o for o in itertools.product(*[range(n) for n in counts]) if any(o)]
        return [far(*o) for o in sorted(offsets, key=hops, reverse=True)]

    sum_phases = (group(1, 1, n_z, 2), group(n_x, n_y, 1, 1))

    barrier = pltpu.get_barrier_semaphore()
    greeted = [neighbour(0, 0, -1), neighbour(0, 0, 1)] + [neighbour(a, b, 0) for a, b in SIDES]
    for d in greeted:
        pl.semaphore_signal(barrier, inc=1, device_id=d, device_id_type=MESH)

    in_copies = []
    for n, (src, dst) in enumerate(
        ((vx_ref, first.at[0, pl.ds(LOW, BX), pl.ds(0, BZ)]),
         (vz_ref, first.at[1, pl.ds(LOW, BX), pl.ds(0, BZ)]),
         (vy_ref, first.at[2, pl.ds(LOW, BX), pl.ds(0, BZ)]),
         (p_ref, first.at[3, pl.ds(LOW, BX), pl.ds(0, BZ)]),
         (ph_ref, ph_in), (vs_in, vs_ref), (pn_in, pn_ref), (dn_in, dn_ref))):
        cp = pltpu.make_async_copy(src, dst, in_sem.at[n])
        cp.start()
        in_copies.append(cp)


    lane_v = lax.broadcasted_iota(jnp.int32, (BZ, BY), 1)
    rows = pl.ds(0, BZ)
    for cp in in_copies:
        cp.wait()
    first[4, LOW:LOW + BX, 0:BZ] = ph_in[...].astype(jnp.float32)

    def pack(k, carry, stores):
        lo = jnp.zeros((BZ, BY), jnp.float32)
        hi = jnp.zeros((BZ, BY), jnp.float32)
        for q in range(2):
            for a in range(5):
                base = GROUP * a + 64 * q
                block = first[a, LOW + 2 * k + q, 0:BZ]
                rolled = pltpu.roll(block, base, 1) if base else block
                lo = jnp.where((lane_v >= base) & (lane_v < base + YHIGH), rolled, lo)
                rolled = pltpu.roll(block, base + SHIFT, 1)
                hi = jnp.where((lane_v >= base + YHIGH) & (lane_v < base + SHIFT), rolled, hi)
        stores += [(s_pack, (0, k), lo), (s_pack, (1, k), hi)]
        return carry

    loop(0, BX // 2, pack, 0, 4)
    pl.semaphore_wait(barrier, len(greeted))

    y_copies = []
    for n, c in enumerate((-1, 1)):
        cp = pltpu.make_async_remote_copy(
            src_ref=s_pack.at[n], dst_ref=r_pack.at[n], send_sem=ysend.at[n], recv_sem=yrecv.at[n],
            device_id=neighbour(0, 0, c), device_id_type=MESH)
        cp.start()
        y_copies.append(cp)

    def exchange(buf, lo, count, send, recv):
        copies = []
        for n, (a, b) in enumerate(SIDES):
            (p0, pn), (r0, rn) = send_planes(a), send_rows(b)
            cp = pltpu.make_async_remote_copy(
                src_ref=buf.at[pl.ds(lo, count), pl.ds(p0, pn), pl.ds(r0, rn)],
                dst_ref=buf.at[pl.ds(lo, count), pl.ds(land_planes(a), pn), pl.ds(land_rows(b), rn)],
                send_sem=send.at[n], recv_sem=recv.at[n],
                device_id=neighbour(a, b, 0), device_id_type=MESH)
            cp.start()
            copies.append(cp)
        return copies

    main_copies = exchange(first, 0, 5, send_a, recv_a)
    for cp in y_copies:
        cp.wait_recv()

    def unpack_y(k, carry, stores):
        both = jnp.where(lax.rem(lax.rem(lane_v, 64), GROUP) >= YHIGH, r_pack[1, k], r_pack[0, k])
        stores.append((first, (5, LOW + 2 * k, rows), both))
        stores.append((first, (5, LOW + 2 * k + 1, rows), pltpu.roll(both, 64, 1)))
        return carry

    loop(0, BX // 2, unpack_y, 0, 8)
    halo_copies = exchange(first, 5, 1, send_b, recv_b)

    full = (ROWS, BY)
    row = lax.broadcasted_iota(jnp.int32, full, 0)
    lane = lax.broadcasted_iota(jnp.int32, full, 1)
    zi = gz * BZ + jnp.where(row >= ROWS - LOW, row - ROWS, row)
    in_strip = jnp.where(lane < YHIGH, lane + BY, jnp.where(lane < BY // 2, lane - SHIFT, lane))
    in_z = (zi >= 0) & (zi < ngz * BZ)
    masks = []
    for cell in (lane, in_strip):
        yi = gy * BY + cell
        in_zy = in_z & (yi >= 0) & (yi < ngy * BY)
        masks.append({None: in_zy, 0: in_zy, 1: in_zy & (zi >= 1), 2: in_zy & (yi >= 1)})

    blank = jnp.zeros(full, jnp.float32)

    def x_ends(part, viscous):
        @pl.when(gx == 0)
        def _():
            for j in range(LOW):
                for a in range(3):
                    vel[part, a, j + 1] = blank
                if viscous:
                    pref[part, j] = blank
            vel[part, 0, LOW + 1] = blank

        @pl.when(gx == ngx - 1)
        def _():
            for j in range(LOW + BX, PLANES):
                for a in range(3):
                    vel[part, a, j + 1] = blank
                if viscous:
                    pref[part, j] = blank

    def splat(ref):
        return [jnp.full(full, ref[k], jnp.float32) for k in range(PHASES)]

    scales, powers, densities = splat(vs_ref), splat(pn_ref), splat(dn_ref)
    powers = [0.5 * (1.0 / n - 1.0) for n in powers]

    def select(phase, table):
        out = table[PHASES - 1]
        for k in range(PHASES - 2, -1, -1):
            out = jnp.where(phase == float(k), table[k], out)
        return out

    def unpack_second(part, j, whole, stores):
        for a in range(3):
            stores.append((vel, (part, a, j + 1), jnp.where(masks[part][a], whole(a, j), 0.0)))
        stores.append((pres, (part, j), whole(3, j)))

    def lookups(part, j, phase, stores):
        stores.append((pref, (part, j), jnp.where(masks[part][None], select(phase, scales), 0.0)))
        stores.append((expo, (part, j), select(phase, powers)))
        stores.append((rho, (part, j), select(phase, densities)))

    def main_first(j, carry, stores):
        unpack_second(0, j, lambda a, j: first[a, j], stores)
        lookups(0, j, first[4, j], stores)
        return carry

    def main_again(j, carry, stores):
        unpack_second(0, j, lambda a, j: second[a, j], stores)
        return carry

    def strip_own(j, carry, stores):
        for a in range(5):
            main = first[a, j]
            own = jnp.where(lane < BY // 2, pltpu.roll(main, SHIFT, 1), main)
            if a < 3:
                stores.append((vel, (1, a, j + 1), own))
            else:
                stores.append((pres if a == 3 else expo, (1, j), own))
        return carry

    def strip_halo(a):
        def body(j, carry, stores):
            halo = first[5, j]
            if a:
                halo = pltpu.roll(halo, BY - GROUP * a, 1)
            halo = jnp.where(lane < SHIFT, halo, vel[1, a, j + 1] if a < 3 else pres[1, j] if a == 3 else expo[1, j])
            if a < 3:
                stores.append((vel, (1, a, j + 1), jnp.where(masks[1][a], halo, 0.0)))
            elif a == 3:
                stores.append((pres, (1, j), halo))
            else:
                lookups(1, j, halo, stores)
            return carry

        return body

    def strip_again(j, carry, stores):
        def left(a, j):
            packed = second[4, j]
            return pltpu.roll(packed, BY - LEFT * a, 1) if a else packed

        unpack_second(1, j, left, stores)
        return carry

    def planes(body):
        loop(0, PLANES, body, 0, UNPACK)

    def iteration(part, first_plane, last_plane):
        def stage(j, carry, stores):
            eta_m, tx_m, vz_m, vy_m, fzx_m, fyx_m, pz_m, py_m, az_m, ay_m, rho_m = carry
            vx, vz, vy = vel[part, 0, j + 1], vel[part, 1, j + 1], vel[part, 2, j + 1]
            rx = vel[part, 0, j + 2] - vx
            rz = z_roll(vz, -1) - vz
            ry = y_roll(vy, -1) - vy
            eta, div = viscosity(rx, rz, ry, pref[part, j], expo[part, j])
            p = pres[part, j] - PRESSURE_STEP * eta * div
            stores.append((pres, (part, j), p))
            tx, tz, ty = eta * rx - p, eta * rz - p, eta * ry - p
            ax = eta + eta_m
            az = eta + z_roll(eta, 1)
            ay = eta + y_roll(eta, 1)
            exz = az + az_m
            exy = ay + ay_m
            eyz = ay + z_roll(ay, 1)
            fzx = exz * (vz - vz_m)
            fyx = exy * (vy - vy_m)
            fxz = exz * (vx - z_roll(vx, 1))
            fxy = exy * (vx - y_roll(vx, 1))
            fyz = eyz * (vy - z_roll(vy, 1))
            fzy = eyz * (vz - y_roll(vz, 1))
            res = tx - tx_m + 0.25 * ((z_roll(fxz, -1) - fxz) + (y_roll(fxy, -1) - fxy))
            new = jnp.where(masks[part][0], vx + (2.0 * VELOCITY_STEP) * res / ax, 0.0)
            stores.append((vel, (part, 0, j + 1), new))
            res = pz_m + 0.25 * (fzx - fzx_m) - rho_m
            new = jnp.where(masks[part][1], vz_m + (2.0 * VELOCITY_STEP) * res / az_m, 0.0)
            stores.append((vel, (part, 1, j), new))
            res = py_m + 0.25 * (fyx - fyx_m)
            new = jnp.where(masks[part][2], vy_m + (2.0 * VELOCITY_STEP) * res / ay_m, 0.0)
            stores.append((vel, (part, 2, j), new))
            pz = tz - z_roll(tz, 1) + 0.25 * (y_roll(fzy, -1) - fzy)
            py = ty - y_roll(ty, 1) + 0.25 * (z_roll(fyz, -1) - fyz)
            return eta, tx, vz, vy, fzx, fyx, pz, py, az, ay, rho[part, j]

        loop(first_plane, last_plane + 1, stage, (blank,) * 11, last_plane + 1 - first_plane)
        x_ends(part, False)

    def odd(part):
        iteration(part, 0, PLANES - 2)

    def even(part):
        iteration(part, 1, PLANES - HIGH)

    def field(part, a, i):
        return vel[part, a, i + LOW + 1, 0:BZ] if a < 3 else pres[part, i + LOW, 0:BZ]

    counted = ((lane_v >= YLOW) & (lane_v < BY - YHIGH), (lane_v >= BY - YHIGH) | ((lane_v >= SHIFT) & (lane_v < SHIFT + YLOW)))

    def last_pressure(part):
        def body(i, total, stores):
            j = i + LOW
            vx = vel[part, 0, j + 1, 0:BZ]
            vz = vel[part, 1, j + 1]
            vy = vel[part, 2, j + 1, 0:BZ]
            rx = vel[part, 0, j + 2, 0:BZ] - vx
            rz = (z_roll(vz, -1) - vz)[0:BZ]
            ry = y_roll(vy, -1) - vy
            eta, div = viscosity(rx, rz, ry, pref[part, j, 0:BZ], expo[part, j, 0:BZ])
            p = pres[part, j, 0:BZ] - PRESSURE_STEP * eta * div
            stores += [(last, (part, 0, i), p), (last, (part, 1, i), eta)]
            return total + jnp.where(counted[part], p, 0.0)

        return body

    for cp in main_copies:
        cp.wait_recv()
    planes(main_first)
    x_ends(0, True)
    odd(0)
    even(0)

    def repack_main(i, carry, stores):
        for a in range(4):
            stores.append((second, (a, i + LOW, rows), field(0, a, i)))
        return carry

    loop(0, BX, repack_main, 0, 8)
    main_second = exchange(second, 0, 4, send_c, recv_c)
    planes(strip_own)

    for cp in halo_copies:
        cp.wait_recv()
    for a in range(5):
        planes(strip_halo(a))
    x_ends(1, True)
    odd(1)
    even(1)

    def repack_strip(i, carry, stores):
        packed = field(1, 0, i)
        place = lane_v + jnp.where(lane_v >= LEFT_AT, -LEFT_AT, BY - LEFT_AT)
        for a in range(1, 4):
            rolled = pltpu.roll(field(1, a, i), LEFT * a, 1)
            packed = jnp.where((place >= LEFT * a) & (place < LEFT * (a + 1)), rolled, packed)
        stores.append((second, (4, i + LOW, rows), packed))
        return carry

    loop(0, BX, repack_strip, 0, 8)
    strip_second_copies = exchange(second, 4, 1, send_d, recv_d)
    for a, b in SIDES:
        pl.semaphore_signal(here.at[0], inc=1, device_id=neighbour(2 * a, 2 * b, 0), device_id_type=MESH)

    for cp in main_second:
        cp.wait_recv()
    planes(main_again)
    x_ends(0, False)
    odd(0)
    total = loop(0, BX, last_pressure(0), jnp.zeros((BZ, BY), jnp.float32), BX)
    for cp in strip_second_copies:
        cp.wait_recv()
    planes(strip_again)
    x_ends(1, False)
    odd(1)

    def joined(main, strip):
        return jnp.where(lane_v < YLOW, pltpu.roll(strip, BY - SHIFT, 1), jnp.where(lane_v >= BY - YHIGH, strip, main))

    total = loop(0, BX, last_pressure(1), total, BX)
    total = jnp.sum(total, axis=0, keepdims=True)
    base = 0
    sum_sends = []
    for n, devices in enumerate(sum_phases):
        count = len(devices)
        ar_src[n] = total
        pl.semaphore_wait(here.at[n], len(SIDES))
        for o, d in enumerate(devices):
            pltpu.make_async_remote_copy(
                src_ref=ar_src.at[n], dst_ref=ar_buf.at[base + o], send_sem=ar_send.at[n], recv_sem=ar_recv.at[n],
                device_id=d, device_id_type=MESH).start()
        part = ar_buf.at[pl.ds(base, count)]
        sum_sends.append(pltpu.make_async_copy(part, part, ar_send.at[n]))
        if n == 0:
            for a, b in SIDES:
                pl.semaphore_signal(here.at[1], inc=1, device_id=neighbour(4 * a, 4 * b, 0), device_id_type=MESH)
            even(0)
            even(1)

            def join(i, carry, stores):
                for a, comp in enumerate((0, 2, 1)):
                    stores.append((out_ref, (a, i), joined(field(0, comp, i), field(1, comp, i))))
                for a in range(2):
                    stores.append((out_ref, (a + 3, i), joined(last[0, a, i], last[1, a, i])))
                return carry

            loop(0, BX, join, 0, 8)
        pltpu.make_async_copy(part, part, ar_recv.at[n]).wait()
        for o in range(count):
            total = total + ar_buf[base + o]
        base += count
    cells = float(ngx * ngy * ngz * BX * BZ * BY)
    mean = jnp.sum(total) / cells
    out_ref[3] = out_ref[3] - mean

    for cp in y_copies + main_copies + halo_copies + main_second + strip_second_copies:
        cp.wait_send()
    for cp in sum_sends:
        cp.wait()


def split_kernel(in_ref, *refs):
    *outs, sem = refs
    copies = [pltpu.make_async_copy(in_ref.at[n], out, sem.at[n]) for n, out in enumerate(outs)]
    for cp in copies:
        cp.start()
    for cp in copies:
        cp.wait()


def local(sizes, vel_x, vel_y, vel_z, pressure, phase, visc_scale, power_n, density):
    ngx, ngy, ngz, z_lo = sizes
    partners = (z_lo * ngy * 2 - 1) + (ngx // z_lo * (ngz // 2) - 1)
    f32 = jnp.float32
    hbm = pl.BlockSpec(memory_space=pltpu.HBM)
    dma = pltpu.SemaphoreType.DMA
    planes = (2, PLANES, ROWS, BY)
    stacked = pl.pallas_call(
        functools.partial(kernel, sizes),
        out_shape=pltpu.VMEM((5, BX, BZ, BY), f32),
        in_specs=[hbm] * 8,
        out_specs=pl.BlockSpec(memory_space=pltpu.VMEM),
        scratch_shapes=[
            pltpu.SMEM((PHASES,), f32),
            pltpu.SMEM((PHASES,), f32),
            pltpu.SMEM((PHASES,), f32),
            pltpu.VMEM((BX, BZ, BY), jnp.int32),
            pltpu.VMEM((6, PLANES, ROWS, BY), f32),
            pltpu.VMEM((5, PLANES, ROWS, BY), f32),
            pltpu.VMEM((2, BX // 2, BZ, BY), f32),
            pltpu.VMEM((2, BX // 2, BZ, BY), f32),
            pltpu.VMEM((2, 3, PLANES + 2, ROWS, BY), f32),
            pltpu.VMEM(planes, f32),
            pltpu.VMEM(planes, f32),
            pltpu.VMEM(planes, f32),
            pltpu.VMEM(planes, f32),
            pltpu.VMEM((2, 2, BX, BZ, BY), f32),
            pltpu.VMEM((2, 1, BY), f32),
            pltpu.VMEM((partners, 1, BY), f32),
            dma((8,)), dma((2,)), dma((2,)),
            dma((8,)), dma((8,)), dma((8,)), dma((8,)), dma((8,)), dma((8,)), dma((8,)), dma((8,)),
            dma((2,)), dma((2,)), pltpu.SemaphoreType.REGULAR((2,)),
        ],
        name="stokes",
        compiler_params=pltpu.CompilerParams(
            collective_id=0, has_side_effects=True, vmem_limit_bytes=VMEM_BYTES),
    )(vel_x, vel_y, vel_z, pressure, phase, visc_scale, power_n, density)
    return pl.pallas_call(
        split_kernel,
        out_shape=[jax.ShapeDtypeStruct((BX, BZ, BY), f32)] * 5,
        in_specs=[pl.BlockSpec(memory_space=pl.ANY)],
        out_specs=[hbm] * 5,
        scratch_shapes=[dma((5,))],
        name="split",
        compiler_params=pltpu.CompilerParams(vmem_limit_bytes=2 * 1024 * 1024),
    )(stacked)


def solution(mesh, z_lo=Z_LO):
    sizes = (mesh.shape["gx"], mesh.shape["gy"], mesh.shape["gz"], z_lo)
    block = P("gx", "gz", "gy")
    return jax.shard_map(
        functools.partial(local, sizes),
        mesh=mesh,
        in_specs=(block,) * 5 + (P(),) * 3,
        out_specs=(block,) * 5,
        check_vma=False,
    )
```
